256 devices in a mesh: cross: 32 (over z, y), along: 8 (over x, core).
Axes of the slice: x: 4, y: 4, z: 8, core: 2. Of those that a mesh axis runs over, the one named last changes fastest.
Arguments:
- source: float32 [16, 128, 8192], P(None, 'along', 'cross'), may hold values from -6 to 6
- inv_density: float32 [16, 128, 8192], P(None, 'along', 'cross'), may hold values from 0.3 to 3
Outputs:
- pressure: float32 [16, 128, 8192], P(None, 'along', 'cross')
- residual: float32 [16, 128, 8192], P(None, 'along', 'cross')
The draws below stay inside these ranges and needn't reach their ends.
All inputs are finite; a program needn't handle non-finite values.
Results may differ from the reference program's by a relative error of at most 0.0003.
Values sent between devices are 32-bit elements; how exact they have to be, the bound alone decides.
A program may use at most 128 MiB of HBM per device.

```python
import math
import jax
import jax.numpy as jnp

NZ = 16
SWEEPS = 4
NX = 128
NY = 8192
LEVELS = 7


def draw_source(key, part):
    key = jax.random.fold_in(key, 7)
    return jnp.clip(jax.random.normal(key, (NZ, NX, NY), jnp.float32), -5.0, 5.0)


def block_levels(stream_key, dims, shards, smallest, top_value):
    level = 1.0
    for position, shards_of in shards:
        steps = jax.random.uniform(jax.random.fold_in(jax.random.fold_in(stream_key, 6), position), (shards_of,), jnp.float32, smallest / len(shards), top_value / len(shards))
        level = level * jnp.repeat(jnp.exp(steps), dims[position] // shards_of).reshape((-1,) + (1,) * (len(dims) - 1 - position))
    return level


def setup_inputs(seed: int = 0) -> dict:
    key_of = jax.random.split(jax.random.key(seed), 3)
    source = draw_source(jax.random.fold_in(key_of[2], 71), 0)
    inv_density = jnp.clip(jnp.exp(math.log(3.0) - 2.3025851 * jax.random.uniform(key_of[1], (NZ, NX, NY), jnp.float32) ** block_levels(key_of[1], (NZ, NX, NY), ((1, 8), (2, 32)), -0.2, 0.2)), 0.3, 3.0)
    return dict(source=source, inv_density=inv_density)


along_weight = 0.25
cross_weight = 1.0
vertical_weight = 0.5
relaxation = 0.8


def harmonic(first, second):
    return 2.0 * first * second / (first + second)


def faces_from(density, padded):
    west_face = along_weight * harmonic(density, padded[:, :-2, 1:-1])
    east_face = along_weight * harmonic(density, padded[:, 2:, 1:-1])
    south_face = cross_weight * harmonic(density, padded[:, 1:-1, :-2])
    north_face = cross_weight * harmonic(density, padded[:, 1:-1, 2:])
    upper_face = jnp.concatenate([2.0 * vertical_weight * density[:1], vertical_weight * harmonic(density[1:], density[:-1])], 0)
    return (west_face, east_face, south_face, north_face, upper_face)


def below_of(upper_face):
    return jnp.concatenate([upper_face[1:], jnp.zeros_like(upper_face[:1])], 0)


def paired(values):
    return values[:, :, 0::2] + values[:, :, 1::2]


def coarsen(face_set):
    west_face, east_face, south_face, north_face, upper_face = face_set
    return (paired(west_face), paired(east_face), 0.5 * south_face[:, :, 0::2], 0.5 * north_face[:, :, 1::2], paired(upper_face))


def centre_of(face_set):
    west_face, east_face, south_face, north_face, upper_face = face_set
    return west_face + east_face + south_face + north_face + upper_face + below_of(upper_face)


def pivots_of(centre, upper_face):
    lower_face = below_of(upper_face)
    pivot_rows = [centre[0]]
    for layer_no in range(1, centre.shape[0]):
        pivot_rows.append(centre[layer_no] - upper_face[layer_no] * lower_face[layer_no - 1] / pivot_rows[-1])
    return jnp.stack(pivot_rows)


def column_solve(pivot_rows, upper_face, remain):
    lower_face = below_of(upper_face)
    layer_count = remain.shape[0]
    forward = [remain[0]]
    for layer_no in range(1, layer_count):
        forward.append(remain[layer_no] + upper_face[layer_no] * forward[-1] / pivot_rows[layer_no - 1])
    result = [None] * layer_count
    result[layer_count - 1] = forward[layer_count - 1] / pivot_rows[layer_count - 1]
    for layer_no in range(layer_count - 2, -1, -1):
        result[layer_no] = (forward[layer_no] + lower_face[layer_no] * result[layer_no + 1]) / pivot_rows[layer_no]
    return jnp.stack(result)


def apply_operator(face_set, centre, current, west_side, east_side, south_side, north_side):
    west_face, east_face, south_face, north_face, upper_face = face_set
    above = jnp.concatenate([jnp.zeros_like(current[:1]), current[:-1]], 0)
    beneath = jnp.concatenate([current[1:], jnp.zeros_like(current[:1])], 0)
    return (centre * current - west_face * west_side - east_face * east_side - south_face * south_side
            - north_face * north_side - upper_face * above - below_of(upper_face) * beneath)


def reference(source, inv_density):
    padded = jnp.pad(inv_density, ((0, 0), (1, 1), (1, 1)))
    face_list = [faces_from(inv_density, padded)]
    for level_no in range(1, LEVELS):
        face_list.append(coarsen(face_list[-1]))
    centre_list = [centre_of(face_set) for face_set in face_list]
    pivot_list = [pivots_of(centre_list[level_no], face_list[level_no][4]) for level_no in range(LEVELS)]

    def operate(level_no, current):
        padded_now = jnp.pad(current, ((0, 0), (1, 1), (1, 1)))
        return apply_operator(face_list[level_no], centre_list[level_no], current,
                              padded_now[:, :-2, 1:-1], padded_now[:, 2:, 1:-1],
                              padded_now[:, 1:-1, :-2], padded_now[:, 1:-1, 2:])

    def smooth(level_no, current, forcing):
        if current is None:
            return relaxation * column_solve(pivot_list[level_no], face_list[level_no][4], forcing)
        remain = forcing - operate(level_no, current)
        return current + relaxation * column_solve(pivot_list[level_no], face_list[level_no][4], remain)

    def cycle(level_no, forcing):
        current = smooth(level_no, None, forcing)
        if level_no == LEVELS - 1:
            for sweep_no in range(SWEEPS - 1):
                current = smooth(level_no, current, forcing)
            return current
        remain = forcing - operate(level_no, current)
        coarse = cycle(level_no + 1, paired(remain))
        current = current + jnp.repeat(coarse, 2, axis=2)
        return smooth(level_no, current, forcing)

    pressure = cycle(0, source)
    return pressure, source - operate(0, pressure)
```

```python
import functools

import jax
import jax.numpy as jnp
from jax import lax
from jax.experimental import pallas as pl
from jax.experimental.pallas import tpu as pltpu
from jax.sharding import PartitionSpec as P

MESH = pl.DeviceIdType.MESH
SWEEPS = 4
NZ = 16
LANES = 128
FINE_ROWS = 32
COARSE_ROWS = 48
TINY = 1e-20

along_weight = 0.25
cross_weight = 1.0
vertical_weight = 0.5
relaxation = 0.8

COARSE_SIDES = [(d, e) for d in (0, 1, -1, 2, -2) for e in (0, 1, -1) if (d, e) != (0, 0)]
FINE_SIDES = [(d, e) for d in (0, 1, -1) for e in (0, 1, -1) if (d, e) != (0, 0)]


def layers(body, init, reverse=False):
    def step(i, carry):
        return body(NZ - 1 - i if reverse else i, carry)

    return lax.fori_loop(0, NZ, step, init, unroll=True)


def picked(values, lane_index):
    return jnp.take_along_axis(values, lane_index, axis=1, mode="promise_in_bounds")


def turned(values, by):
    return pltpu.roll(values, by % LANES, axis=1)


def row_turned(values, by):
    return pltpu.roll(values, by % values.shape[0], axis=0)


def harmonic(first, second):
    return 2.0 * first * second / jnp.maximum(first + second, TINY)


def lanes_of(rows):
    return lax.broadcasted_iota(jnp.int32, (rows, LANES), 1)


class Level:
    def __init__(self, phases, spread, rows, refs):
        self.phases, self.spread, self.rows = phases, spread, rows
        self.west, self.east, self.south, self.last_north, self.upper, self.inverse, self.link, self.value, self.forcing = refs

    @staticmethod
    def scratch(phases, rows):
        full = pltpu.VMEM((phases, NZ, rows, LANES), jnp.float32)
        return [
            full,
            full,
            full,
            pltpu.VMEM((NZ, rows, LANES), jnp.float32),
            pltpu.VMEM((phases, NZ + 1, rows, LANES), jnp.float32),
            full,
            full,
            full,
            full,
        ]

    def north(self, phase, k):
        return self.south[phase + 1, k] if phase + 1 < self.phases else self.last_north[k]

    def horizontal(self, k, values):
        out = []
        for phase, value in enumerate(values):
            before = values[phase - 1] if phase else turned(values[-1], self.spread)
            after = values[phase + 1] if phase + 1 < self.phases else turned(values[0], -self.spread)
            out.append(
                self.west[phase, k] * row_turned(value, 1)
                + self.east[phase, k] * row_turned(value, -1)
                + self.south[phase, k] * before
                + self.north(phase, k) * after
            )
        return out

    def set_faces(self, k, west, south, upper):
        for phase in range(self.phases):
            self.west[phase, k] = west[phase]
            self.east[phase, k] = row_turned(west[phase], -1)
            self.south[phase, k] = south[phase]
            self.upper[phase, k] = upper[phase]
        self.last_north[k] = turned(south[0], -self.spread)

    def close_upper(self):
        for phase in range(self.phases):
            self.upper[phase, NZ] = jnp.zeros((self.rows, LANES), jnp.float32)

    def factor(self, centre_ref=None):
        def body(k, before):
            now = []
            for phase in range(self.phases):
                upper, lower = self.upper[phase, k], self.upper[phase, k + 1]
                centre = self.west[phase, k] + self.east[phase, k] + self.south[phase, k] + self.north(phase, k) + upper + lower
                if centre_ref is not None:
                    centre_ref[phase, k] = centre
                inverse = 1.0 / jnp.maximum(centre - upper * upper * before[phase], TINY)
                self.inverse[phase, k] = inverse
                self.link[phase, k] = lower * inverse
                now.append(inverse)
            return tuple(now)

        zero = jnp.zeros((self.rows, LANES), jnp.float32)
        layers(body, (zero,) * self.phases)

    def start(self, held, after=None, low=0):
        rows = pl.ds(low, self.rows - low)
        zero = jnp.zeros((self.rows - low, LANES), jnp.float32)

        def down(k, before):
            now = []
            for phase in range(self.phases):
                total = self.forcing[phase, k, rows] + self.upper[phase, k, rows] * before[phase]
                now.append(total * self.inverse[phase, k, rows])
                held[phase, k, rows] = now[-1]
            return tuple(now)

        layers(down, (zero,) * self.phases)

        def up(k, below):
            now, values = [], []
            for phase in range(self.phases):
                now.append(held[phase, k, rows] + self.link[phase, k, rows] * below[phase])
                values.append(relaxation * now[-1])
                self.value[phase, k, rows] = values[-1]
            if after is not None:
                after(k, values)
            return tuple(now)

        layers(up, (zero,) * self.phases, reverse=True)

    def remain(self, k, values):
        return [(1.0 - relaxation) * self.forcing[phase, k] + part for phase, part in enumerate(self.horizontal(k, values))]

    def sweep(self, held, coarse=None):
        zero = jnp.zeros((self.rows, LANES), jnp.float32)

        def down(k, before):
            values = [self.value[phase, k] for phase in range(self.phases)]
            if coarse is not None:
                values = [value + extra for value, extra in zip(values, coarse(k))]
                for phase in range(self.phases):
                    self.value[phase, k] = values[phase]
            now = []
            for phase, part in enumerate(self.horizontal(k, values)):
                total = self.forcing[phase, k] + part + self.upper[phase, k] * before[phase]
                now.append(total * self.inverse[phase, k])
                held[phase, k] = now[-1]
            return tuple(now)

        layers(down, (zero,) * self.phases)

        def up(k, below):
            now = []
            for phase in range(self.phases):
                now.append(held[phase, k] + self.link[phase, k] * below[phase])
                self.value[phase, k] = (1.0 - relaxation) * self.value[phase, k] + relaxation * now[-1]
            return tuple(now)

        layers(up, (zero,) * self.phases, reverse=True)


def paired_lanes(values, spread, lane):
    return values + picked(values, lane ^ spread)


def first_child(values, spread, lane):
    return jnp.where((lane & spread) == 0, values, turned(values, spread))


def kernel(
    cross_count,
    along_count,
    source_ref,
    density_ref,
    pressure_ref,
    residual_ref,
    dense,
    first_out,
    last_out,
    first_in,
    last_in,
    near_out,
    far_out,
    own_in,
    near_in,
    far_in,
    fresh,
    cells,
    centre,
    held,
    coarse_held,
    *rest,
):
    level_refs, (fine_send, fine_recv, coarse_send, coarse_recv, fresh_send, fresh_recv) = rest[:-6], rest[-6:]
    shapes = [(4, 1, FINE_ROWS), (2, 1, FINE_ROWS), (1, 1, FINE_ROWS), (1, 2, FINE_ROWS), (1, 1, COARSE_ROWS), (1, 2, COARSE_ROWS), (1, 4, COARSE_ROWS)]
    grid = [Level(*shape, level_refs[9 * no : 9 * no + 9]) for no, shape in enumerate(shapes)]
    c, a = lax.axis_index("cross"), lax.axis_index("along")

    def inside(d, e):
        return (c + d >= 0) & (c + d < cross_count) & (a + e >= 0) & (a + e < along_count)

    for ref in (first_in, last_in, own_in, near_in, far_in, fresh):
        ref[...] = jnp.zeros(ref.shape, ref.dtype)
    dense[:, :, :, 16:32, :] = jnp.zeros((2, 2, NZ, 16, LANES), jnp.float32)

    barrier = pltpu.get_barrier_semaphore()
    for d, e in COARSE_SIDES:

        @pl.when(inside(d, e))
        def _(d=d, e=e):
            pl.semaphore_signal(barrier, inc=1, device_id=(c + d, a + e), device_id_type=MESH)

    def own_cells(which, ref):
        lane = lanes_of(16)
        index = (4 * (lane & 63) + (lane >> 6)) & 127
        lower = (lane & 63) < 32

        def body(k, _):
            left, right = ref[k, :, 0:LANES], ref[k, :, LANES : 2 * LANES]
            for half in range(2):
                at = index + 2 * half
                dense[which, half, k, 0:16] = jnp.where(lower, picked(left, at), picked(right, at))
            return 0

        layers(body, 0)
        slot = (lane & 63) >> 3
        for half in range(2):
            for group in range(2):
                first = last = jnp.zeros((16, LANES), jnp.float32)
                for q in range(8):
                    values = dense[which, half, 8 * group + q, 0:16]
                    first = jnp.where(slot == q, turned(values, 8 * q), first)
                    last = jnp.where(slot == q, turned(values, 8 * q + 72), last)
                first_out[which, half, group] = first
                last_out[which, half, group] = last

    def fine_copies(which):
        copies = []
        for no, (d, e) in enumerate(FINE_SIDES):
            rows_from = {0: (0, 16), 1: (0, 8), -1: (8, 16)}[e]
            rows_to = {0: (0, 16), 1: (16, 24), -1: (24, 32)}[e]
            take, put = pl.ds(rows_from[0], rows_from[1] - rows_from[0]), pl.ds(rows_to[0], rows_to[1] - rows_to[0])
            if d == 0:
                src, dst = dense.at[which, :, :, take, :], dense.at[which, :, :, put, :]
            elif d == 1:
                src, dst = first_out.at[which, :, :, take, :], first_in.at[which, :, :, put, :]
            else:
                src, dst = last_out.at[which, :, :, take, :], last_in.at[which, :, :, put, :]
            copies.append(
                (
                    d,
                    e,
                    pltpu.make_async_remote_copy(
                        src_ref=src,
                        dst_ref=dst,
                        send_sem=fine_send.at[which, no],
                        recv_sem=fine_recv.at[which, no],
                        device_id=(c - d, a - e),
                        device_id_type=MESH,
                    ),
                )
            )
        return copies

    def coarse_copies(which):
        fields = pl.ds(0, 3) if which == 0 else pl.ds(3, 1)
        copies = []
        for no, (d, e) in enumerate(COARSE_SIDES):
            put = pl.ds({0: 0, 1: 16, -1: 32}[e], 16)
            if d == 0:
                src, dst = own_in.at[fields, :, pl.ds(0, 16), :], own_in.at[fields, :, put, :]
            elif abs(d) == 1:
                side = 0 if d > 0 else 1
                src, dst = near_out.at[side, fields], near_in.at[side, fields, :, put, :]
            else:
                side = 0 if d > 0 else 1
                src, dst = far_out.at[fields], far_in.at[side, fields, put, :]
            copies.append(
                (
                    d,
                    e,
                    pltpu.make_async_remote_copy(
                        src_ref=src,
                        dst_ref=dst,
                        send_sem=coarse_send.at[which, no],
                        recv_sem=coarse_recv.at[which, no],
                        device_id=(c - d, a - e),
                        device_id_type=MESH,
                    ),
                )
            )
        return copies

    def fresh_copies():
        copies = []
        for no, (e, take) in enumerate([(1, 0), (-1, 8)]):
            copies.append(
                (
                    0,
                    e,
                    pltpu.make_async_remote_copy(
                        src_ref=grid[3].forcing.at[0, :, pl.ds(take, 8), :],
                        dst_ref=fresh.at[no],
                        send_sem=fresh_send.at[no],
                        recv_sem=fresh_recv.at[no],
                        device_id=(c, a - e),
                        device_id_type=MESH,
                    ),
                )
            )
        return copies

    def start(copies):
        for d, e, copy in copies:
            pl.when(inside(-d, -e))(copy.start)

    def arrive(copies):
        for d, e, copy in copies:
            pl.when(inside(d, e))(copy.wait_recv)

    def leave(copies):
        for d, e, copy in copies:
            pl.when(inside(-d, -e))(copy.wait_send)

    def whole_cells(which, target):
        lane = lanes_of(FINE_ROWS)
        own = lane < 64
        for group in range(2):
            halos = []
            for phase in range(4):
                first, last = first_in[which, phase // 2, group], last_in[which, phase // 2, group]
                if phase % 2 == 0:
                    halos.append(jnp.where(own, first, turned(last, 64)))
                else:
                    halos.append(jnp.where(own, turned(first, 64), last))

            def body(q, halos, group=group):
                index = jnp.where(lane < 96, (lane + 8 * q) & 63, 64 + ((lane + 8 + 8 * q) & 63))
                k = 8 * group + q
                for phase in range(4):
                    values = dense[which, phase // 2, k]
                    if phase % 2:
                        values = turned(values, 64)
                    target[phase, k] = jnp.where(own, values, picked(halos[phase], index))
                return halos

            lax.fori_loop(0, 8, body, tuple(halos), unroll=True)

    own_cells(1, density_ref)
    counted = (
        (jnp.minimum(c, 2) + jnp.minimum(cross_count - 1 - c, 2) + 1) * (jnp.minimum(a, 1) + jnp.minimum(along_count - 1 - a, 1) + 1) - 1
    )
    pl.semaphore_wait(barrier, counted)
    density_copies = fine_copies(1)
    start(density_copies)
    own_cells(0, source_ref)
    source_copies = fine_copies(0)
    start(source_copies)
    for level in grid:
        level.close_upper()
    arrive(density_copies)
    whole_cells(1, cells)

    lane = lanes_of(FINE_ROWS)
    lane_16 = lanes_of(16)

    def faces(k, above):
        now = [cells[phase, k] for phase in range(4)]
        west, south, upper = [], [], []
        for phase in range(4):
            before = now[phase - 1] if phase else turned(now[3], 1)
            west.append(along_weight * harmonic(now[phase], row_turned(now[phase], 1)))
            south.append(cross_weight * harmonic(now[phase], before))
            upper.append(vertical_weight * harmonic(now[phase], above[phase]))
        upper = [jnp.where(k == 0, 2.0 * vertical_weight * now[phase], upper[phase]) for phase in range(4)]
        grid[0].set_faces(k, west, south, upper)
        west, south, upper = [west[0] + west[1], west[2] + west[3]], [0.5 * south[0], 0.5 * south[2]], [upper[0] + upper[1], upper[2] + upper[3]]
        grid[1].set_faces(k, west, south, upper)
        west, south, upper = [west[0] + west[1]], [0.5 * south[0]], [upper[0] + upper[1]]
        grid[2].set_faces(k, west, south, upper)
        west, south, upper = paired_lanes(west[0], 1, lane), 0.5 * first_child(south[0], 1, lane), paired_lanes(upper[0], 1, lane)
        grid[3].set_faces(k, [west], [south], [upper])
        return tuple(now)

    layers(faces, (jnp.ones((FINE_ROWS, LANES), jnp.float32),) * 4)

    def pack(field, layer_of):
        near_index = 4 * (lane_16 & 15)
        far_index = 4 * ((lane_16 & 3) + 12 * (lane_16 >> 6))
        near_slot, far_slot = lane_16 >> 4, (lane_16 & 63) >> 2
        far = jnp.zeros((16, LANES), jnp.float32)
        for group in range(2):
            near = jnp.zeros((16, LANES), jnp.float32)
            for q in range(8):
                k = 8 * group + q
                value = layer_of(k)
                near = jnp.where(near_slot == q, value(near_index), near)
                far = jnp.where(far_slot == k, value(far_index), far)
            own_in[field, group, 0:16] = near
            near_out[0, field, group] = turned(near, 16)
            near_out[1, field, group] = turned(near, -16)
        far_out[field] = far

    def both(ref):
        def layer_of(k):
            values = ref[0, k, 0:16]
            return lambda index: picked(values, index) + picked(values, index + 2)

        return layer_of

    def half_first(ref):
        def layer_of(k):
            values = ref[0, k, 0:16]
            return lambda index: 0.5 * picked(values, index)

        return layer_of

    pack(0, both(grid[3].west))
    pack(1, half_first(grid[3].south))
    pack(2, both(grid[3].upper))
    face_copies = coarse_copies(0)
    start(face_copies)

    grid[0].factor(centre)
    for no in (1, 2, 3):
        grid[no].factor()

    arrive(source_copies)
    whole_cells(0, grid[0].forcing)

    def restrict(no):
        level, below = grid[no], grid[no + 1]

        def after(k, values):
            rest = level.remain(k, values)
            if level.phases > 1:
                for phase in range(below.phases):
                    below.forcing[phase, k] = rest[2 * phase] + rest[2 * phase + 1]
            else:
                below.forcing[0, k] = paired_lanes(rest[0], level.spread, lanes_of(level.rows))

        return after

    for no in (0, 1, 2):
        grid[no].start(held, restrict(no))
    third_copies = fresh_copies()
    start(third_copies)

    def keep_rest(k, values):
        cells[0, k] = grid[3].remain(k, values)[0]

    grid[3].start(held, keep_rest)
    pack(3, both(cells))
    forcing_copies = coarse_copies(1)
    start(forcing_copies)

    arrive(third_copies)

    def renew(k, _):
        grid[3].forcing[0, k, 16:24] = fresh[0, k]
        grid[3].forcing[0, k, 24:32] = fresh[1, k]
        return 0

    layers(renew, 0)
    grid[3].start(held, low=16)

    lane_48 = lanes_of(COARSE_ROWS)

    def unpacked(field):
        near_slot = lane_48 >> 4
        middle = (lane_48 >= 32) & (lane_48 < 112)
        far = jnp.where(lane_48 < 64, far_in[0, field], far_in[1, field])

        def layer_of(k):
            group, q = k // 8, k % 8
            mixed = jnp.where(
                near_slot == q,
                own_in[field, group],
                jnp.where(near_slot == (q + 1) % 8, near_in[0, field, group], near_in[1, field, group]),
            )
            index = jnp.where(lane_48 < 64, (4 * k + lane_48 + 32) & 63, 64 + ((4 * k + lane_48 + 20) & 63))
            return jnp.where(middle, picked(far, index), turned(mixed, -16 * q))

        return layer_of

    arrive(face_copies)
    west_of, south_of, upper_of = unpacked(0), unpacked(1), unpacked(2)
    for k in range(NZ):
        west, south, upper = west_of(k), south_of(k), upper_of(k)
        grid[4].set_faces(k, [west], [south], [upper])
        for no in (5, 6):
            spread = grid[no].spread // 2
            west, south, upper = paired_lanes(west, spread, lane_48), 0.5 * first_child(south, spread, lane_48), paired_lanes(upper, spread, lane_48)
            grid[no].set_faces(k, [west], [south], [upper])
    for no in (4, 5, 6):
        grid[no].factor()

    arrive(forcing_copies)
    forcing_of = unpacked(3)
    for k in range(NZ):
        grid[4].forcing[0, k] = forcing_of(k)

    grid[4].start(coarse_held, restrict(4))
    grid[5].start(coarse_held, restrict(5))
    grid[6].start(coarse_held)
    for _ in range(SWEEPS - 1):
        grid[6].sweep(coarse_held)
    grid[5].sweep(coarse_held, lambda k: [grid[6].value[0, k]])
    grid[4].sweep(coarse_held, lambda k: [grid[5].value[0, k]])

    def to_third(k):
        values = jnp.concatenate([grid[4].value[0, k, 0:24], grid[4].value[0, k, 40:48]], 0)
        return [picked(values, jnp.where(lane < 96, lane >> 2, (lane >> 2) + 96))]

    grid[3].sweep(held, to_third)
    grid[2].sweep(held, lambda k: [grid[3].value[0, k]])
    grid[1].sweep(held, lambda k: [grid[2].value[0, k]] * 2)
    grid[0].sweep(held, lambda k: [grid[1].value[phase // 2, k] for phase in range(4)])

    def laid_out(ref, k, phases):
        halves = [jnp.where(lane_16 < 64, phases[2 * half], turned(phases[2 * half + 1], 64)) for half in range(2)]
        index = (lane_16 & 1) * 64 + (lane_16 >> 2)
        for tile in range(2):
            at = index + 32 * tile
            ref[k, :, tile * LANES : (tile + 1) * LANES] = jnp.where((lane_16 & 3) < 2, picked(halves[0], at), picked(halves[1], at))

    fine = grid[0]

    def finish(k, above):
        values = [fine.value[phase, k] for phase in range(4)]
        next_k = jnp.minimum(k + 1, NZ - 1)
        rest = []
        for phase, part in enumerate(fine.horizontal(k, values)):
            own = pl.ds(0, 16)
            below = fine.value[phase, next_k, own]
            rest.append(
                fine.forcing[phase, k, own]
                - (
                    centre[phase, k, own] * values[phase][0:16]
                    - part[0:16]
                    - fine.upper[phase, k, own] * above[phase]
                    - fine.upper[phase, k + 1, own] * below
                )
            )
        values = [value[0:16] for value in values]
        laid_out(pressure_ref, k, values)
        laid_out(residual_ref, k, rest)
        return tuple(values)

    layers(finish, (jnp.zeros((16, LANES), jnp.float32),) * 4)

    for copies in (density_copies, source_copies, face_copies, third_copies, forcing_copies):
        leave(copies)


def solution(mesh):
    cross_count, along_count = mesh.shape["cross"], mesh.shape["along"]

    def per_device(source, density):
        shape = jax.ShapeDtypeStruct(source.shape, jnp.float32)
        vmem = lambda *dims: pltpu.VMEM(dims, jnp.float32)
        scratch = [
            vmem(2, 2, NZ, FINE_ROWS, LANES),
            vmem(2, 2, 2, 16, LANES),
            vmem(2, 2, 2, 16, LANES),
            vmem(2, 2, 2, FINE_ROWS, LANES),
            vmem(2, 2, 2, FINE_ROWS, LANES),
            vmem(2, 4, 2, 16, LANES),
            vmem(4, 16, LANES),
            vmem(4, 2, COARSE_ROWS, LANES),
            vmem(2, 4, 2, COARSE_ROWS, LANES),
            vmem(2, 4, COARSE_ROWS, LANES),
            vmem(2, NZ, 8, LANES),
            vmem(4, NZ, FINE_ROWS, LANES),
            vmem(4, NZ, FINE_ROWS, LANES),
            vmem(4, NZ, FINE_ROWS, LANES),
            vmem(1, NZ, COARSE_ROWS, LANES),
        ]
        for phases, rows in [(4, FINE_ROWS), (2, FINE_ROWS), (1, FINE_ROWS), (1, FINE_ROWS)] + [(1, COARSE_ROWS)] * 3:
            scratch += Level.scratch(phases, rows)
        scratch += [
            pltpu.SemaphoreType.DMA((2, len(FINE_SIDES))),
            pltpu.SemaphoreType.DMA((2, len(FINE_SIDES))),
            pltpu.SemaphoreType.DMA((2, len(COARSE_SIDES))),
            pltpu.SemaphoreType.DMA((2, len(COARSE_SIDES))),
            pltpu.SemaphoreType.DMA((2,)),
            pltpu.SemaphoreType.DMA((2,)),
        ]
        return pl.pallas_call(
            functools.partial(kernel, cross_count, along_count),
            out_shape=(shape, shape),
            in_specs=[pl.BlockSpec(memory_space=pltpu.VMEM)] * 2,
            out_specs=(pl.BlockSpec(memory_space=pltpu.VMEM),) * 2,
            scratch_shapes=scratch,
            compiler_params=pltpu.CompilerParams(collective_id=0, has_side_effects=True, vmem_limit_bytes=56 * 2**20),
        )(source, density)

    return jax.shard_map(
        per_device,
        mesh=mesh,
        in_specs=(P(None, "along", "cross"), P(None, "along", "cross")),
        out_specs=(P(None, "along", "cross"), P(None, "along", "cross")),
        check_vma=False,
    )
```

```python
import functools

import jax
import jax.numpy as jnp
from jax import lax
from jax.experimental import pallas as pl
from jax.experimental.pallas import tpu as pltpu
from jax.sharding import PartitionSpec as P

MESH = pl.DeviceIdType.MESH
SWEEPS = 4
NZ = 16
LANES = 128
FINE_ROWS = 32
COARSE_ROWS = 24
HELD_ROWS = 48
TINY = 1e-20

along_weight = 0.25
cross_weight = 1.0
vertical_weight = 0.5
relaxation = 0.8

COARSE_SIDES = [(d, e) for d in (0, 1, -1, 2, -2) for e in (0, 1, -1) if (d, e) != (0, 0)]
FINE_SIDES = [(d, e) for d in (0, 1, -1) for e in (0, 1, -1) if (d, e) != (0, 0)]


def layers(body, init, reverse=False):
    def step(i, carry):
        return body(NZ - 1 - i if reverse else i, carry)

    return lax.fori_loop(0, NZ, step, init, unroll=True)


def picked(values, lane_index):
    return jnp.take_along_axis(values, lane_index, axis=1, mode="promise_in_bounds")


def turned(values, by):
    return pltpu.roll(values, by % LANES, axis=1)


def row_turned(values, by):
    return pltpu.roll(values, by % values.shape[0], axis=0)


def harmonic(first, second):
    return 2.0 * first * second / jnp.maximum(first + second, TINY)


def lanes_of(rows):
    return lax.broadcasted_iota(jnp.int32, (rows, LANES), 1)


def row_before(values, folded):
    moved = row_turned(values, 1)
    if not folded:
        return moved
    head = moved[0:8]
    first = lax.broadcasted_iota(jnp.int32, head.shape, 0) == 0
    return jnp.concatenate([jnp.where(first, turned(head, 64), head), moved[8:]], 0)


def row_after(values, folded):
    moved = row_turned(values, -1)
    if not folded:
        return moved
    tail = moved[-8:]
    last = lax.broadcasted_iota(jnp.int32, tail.shape, 0) == 7
    return jnp.concatenate([moved[:-8], jnp.where(last, turned(tail, 64), tail)], 0)


class Level:
    def __init__(self, phases, spread, rows, refs):
        self.phases, self.spread, self.rows, self.folded = phases, spread, rows, rows == COARSE_ROWS
        self.west, self.east, self.south, self.last_north, self.upper, self.gain, self.pull, self.link, self.value, self.forcing = refs

    @staticmethod
    def scratch(phases, rows):
        full = pltpu.VMEM((phases, NZ, rows, LANES), jnp.float32)
        edge = pltpu.VMEM((NZ, rows, LANES), jnp.float32)
        column = pltpu.VMEM((phases, NZ + 1, rows, LANES), jnp.float32)
        return [full, full, full, edge, column, full, full, full, full, full]

    def north(self, phase, k):
        return self.south[phase + 1, k] if phase + 1 < self.phases else self.last_north[k]

    def horizontal(self, k, values):
        out = []
        for phase, value in enumerate(values):
            before = values[phase - 1] if phase else turned(values[-1], self.spread)
            after = values[phase + 1] if phase + 1 < self.phases else turned(values[0], -self.spread)
            out.append(
                self.west[phase, k] * row_before(value, self.folded)
                + self.east[phase, k] * row_after(value, self.folded)
                + self.south[phase, k] * before
                + self.north(phase, k) * after
            )
        return out

    def set_faces(self, k, west, south, upper):
        for phase in range(self.phases):
            self.west[phase, k] = west[phase]
            self.east[phase, k] = row_after(west[phase], self.folded)
            self.south[phase, k] = south[phase]
            self.upper[phase, k] = upper[phase]
        self.last_north[k] = turned(south[0], -self.spread)

    def close_upper(self):
        for phase in range(self.phases):
            self.upper[phase, NZ] = jnp.zeros((self.rows, LANES), jnp.float32)

    def start(self, held, after=None, low=0):
        rows = pl.ds(low, self.rows - low)
        zero = jnp.zeros((self.rows - low, LANES), jnp.float32)

        def down(k, before):
            now = []
            for phase in range(self.phases):
                now.append(self.gain[phase, k, rows] * self.forcing[phase, k, rows] + self.pull[phase, k, rows] * before[phase])
                held[phase, k, rows] = now[-1]
            return tuple(now)

        layers(down, (zero,) * self.phases)

        def up(k, below):
            values = []
            for phase in range(self.phases):
                values.append(held[phase, k, rows] + self.link[phase, k, rows] * below[phase])
                self.value[phase, k, rows] = values[-1]
            if after is not None:
                after(k, values)
            return tuple(values)

        layers(up, (zero,) * self.phases, reverse=True)

    def remain(self, k, values):
        return [(1.0 - relaxation) * self.forcing[phase, k] + part for phase, part in enumerate(self.horizontal(k, values))]

    def sweep(self, held, coarse=None):
        zero = jnp.zeros((self.rows, LANES), jnp.float32)

        def down(k, before):
            values = [self.value[phase, k] for phase in range(self.phases)]
            if coarse is not None:
                values = [value + extra for value, extra in zip(values, coarse(k))]
                for phase in range(self.phases):
                    self.value[phase, k] = values[phase]
            now = []
            for phase, part in enumerate(self.horizontal(k, values)):
                now.append(self.gain[phase, k] * (self.forcing[phase, k] + part) + self.pull[phase, k] * before[phase])
                held[phase, k] = now[-1]
            return tuple(now)

        layers(down, (zero,) * self.phases)

        def up(k, below):
            now = []
            for phase in range(self.phases):
                now.append(held[phase, k] + self.link[phase, k] * below[phase])
                self.value[phase, k] = (1.0 - relaxation) * self.value[phase, k] + now[-1]
            return tuple(now)

        layers(up, (zero,) * self.phases, reverse=True)


def factor(levels, centre_ref=None):
    def body(k, before):
        now = []
        for no, level in enumerate(levels):
            links = []
            for phase in range(level.phases):
                upper, lower = level.upper[phase, k], level.upper[phase, k + 1]
                centre = level.west[phase, k] + level.east[phase, k] + level.south[phase, k] + level.north(phase, k) + upper + lower
                if no == 0 and centre_ref is not None:
                    centre_ref[phase, k] = centre
                inverse = 1.0 / jnp.maximum(centre - upper * before[no][phase], TINY)
                level.gain[phase, k] = relaxation * inverse
                level.pull[phase, k] = upper * inverse
                links.append(lower * inverse)
                level.link[phase, k] = links[-1]
            now.append(tuple(links))
        return tuple(now)

    layers(body, tuple((jnp.zeros((level.rows, LANES), jnp.float32),) * level.phases for level in levels))


def paired_lanes(values, spread, lane):
    return values + picked(values, lane ^ spread)


def first_child(values, spread, lane):
    return jnp.where((lane & spread) == 0, values, turned(values, spread))


def kernel(
    cross_count,
    along_count,
    source_hbm,
    density_hbm,
    pressure_hbm,
    residual_hbm,
    raw,
    dense,
    first_out,
    last_out,
    first_in,
    last_in,
    near_out,
    far_out,
    own_in,
    near_in,
    far_in,
    fresh,
    cells,
    centre,
    held,
    coarse_held,
    *rest,
):
    level_refs, (own_sem, out_sem, fine_send, fine_recv, coarse_send, coarse_recv, fresh_send, fresh_recv) = rest[:-8], rest[-8:]
    shapes = [(4, 1, FINE_ROWS), (2, 1, FINE_ROWS), (1, 1, FINE_ROWS), (1, 2, FINE_ROWS), (1, 1, COARSE_ROWS), (1, 2, COARSE_ROWS), (1, 4, COARSE_ROWS)]
    grid = [Level(*shape, level_refs[10 * no : 10 * no + 10]) for no, shape in enumerate(shapes)]
    c, a = lax.axis_index("cross"), lax.axis_index("along")

    def inside(d, e):
        return (c + d >= 0) & (c + d < cross_count) & (a + e >= 0) & (a + e < along_count)

    own_copies = [pltpu.make_async_copy(hbm, raw.at[which], own_sem.at[which]) for which, hbm in ((0, source_hbm), (1, density_hbm))]
    for copy in own_copies[::-1]:
        copy.start()

    for ref in (first_in, last_in, own_in, near_in, far_in, fresh):
        ref[...] = jnp.zeros(ref.shape, ref.dtype)
    dense[:, :, :, 16:32, :] = jnp.zeros((2, 2, NZ, 16, LANES), jnp.float32)

    barrier = pltpu.get_barrier_semaphore()
    for d, e in COARSE_SIDES:

        @pl.when(inside(d, e))
        def _(d=d, e=e):
            pl.semaphore_signal(barrier, inc=1, device_id=(c + d, a + e), device_id_type=MESH)

    def own_cells(which):
        own_copies[which].wait()
        ref = raw.at[which]
        lane = lanes_of(16)
        index = (4 * (lane & 63) + (lane >> 6)) & 127
        lower = (lane & 63) < 32

        def body(k, _):
            left, right = ref[k, :, 0:LANES], ref[k, :, LANES : 2 * LANES]
            for half in range(2):
                at = index + 2 * half
                dense[which, half, k, 0:16] = jnp.where(lower, picked(left, at), picked(right, at))
            return 0

        layers(body, 0)
        slot = (lane & 63) >> 3
        for half in range(2):
            for group in range(2):
                first = last = jnp.zeros((16, LANES), jnp.float32)
                for q in range(8):
                    values = dense[which, half, 8 * group + q, 0:16]
                    first = jnp.where(slot == q, turned(values, 8 * q), first)
                    last = jnp.where(slot == q, turned(values, 8 * q + 72), last)
                first_out[which, half, group] = first
                last_out[which, half, group] = last

    def fine_copies(which):
        copies = []
        for no, (d, e) in enumerate(FINE_SIDES):
            rows_from = {0: (0, 16), 1: (0, 8), -1: (8, 16)}[e]
            rows_to = {0: (0, 16), 1: (16, 24), -1: (24, 32)}[e]
            take, put = pl.ds(rows_from[0], rows_from[1] - rows_from[0]), pl.ds(rows_to[0], rows_to[1] - rows_to[0])
            if d == 0:
                src, dst = dense.at[which, :, :, take, :], dense.at[which, :, :, put, :]
            elif d == 1:
                src, dst = first_out.at[which, :, :, take, :], first_in.at[which, :, :, put, :]
            else:
                src, dst = last_out.at[which, :, :, take, :], last_in.at[which, :, :, put, :]
            copies.append(
                (
                    d,
                    e,
                    pltpu.make_async_remote_copy(
                        src_ref=src,
                        dst_ref=dst,
                        send_sem=fine_send.at[which, no],
                        recv_sem=fine_recv.at[which, no],
                        device_id=(c - d, a - e),
                        device_id_type=MESH,
                    ),
                )
            )
        return copies

    def coarse_copies(which):
        fields = (pl.ds(2, 1), pl.ds(0, 2), pl.ds(3, 1))[which]
        copies = []
        for no, (d, e) in enumerate(COARSE_SIDES):
            put = pl.ds({0: 0, 1: 16, -1: 32}[e], 16)
            if d == 0:
                src, dst = own_in.at[fields, :, pl.ds(0, 16), :], own_in.at[fields, :, put, :]
            elif abs(d) == 1:
                side = 0 if d > 0 else 1
                src, dst = near_out.at[side, fields], near_in.at[side, fields, :, put, :]
            else:
                side = 0 if d > 0 else 1
                src, dst = far_out.at[side, fields], far_in.at[side, {0: 0, 1: 1, -1: 2}[e], fields]
            copies.append(
                (
                    d,
                    e,
                    pltpu.make_async_remote_copy(
                        src_ref=src,
                        dst_ref=dst,
                        send_sem=coarse_send.at[which, no],
                        recv_sem=coarse_recv.at[which, no],
                        device_id=(c - d, a - e),
                        device_id_type=MESH,
                    ),
                )
            )
        return copies

    def fresh_copies():
        copies = []
        for no, (e, take) in enumerate([(1, 0), (-1, 8)]):
            copies.append(
                (
                    0,
                    e,
                    pltpu.make_async_remote_copy(
                        src_ref=grid[3].forcing.at[0, :, pl.ds(take, 8), :],
                        dst_ref=fresh.at[no],
                        send_sem=fresh_send.at[no],
                        recv_sem=fresh_recv.at[no],
                        device_id=(c, a - e),
                        device_id_type=MESH,
                    ),
                )
            )
        return copies

    def start(copies):
        for d, e, copy in copies:
            pl.when(inside(-d, -e))(copy.start)

    def arrive(copies):
        for d, e, copy in copies:
            pl.when(inside(d, e))(copy.wait_recv)

    def leave(copies):
        for d, e, copy in copies:
            pl.when(inside(-d, -e))(copy.wait_send)

    def whole_cells(which, target):
        lane = lanes_of(FINE_ROWS)
        own = lane < 64
        for group in range(2):
            halos = []
            for phase in range(4):
                first, last = first_in[which, phase // 2, group], last_in[which, phase // 2, group]
                if phase % 2 == 0:
                    halos.append(jnp.where(own, first, turned(last, 64)))
                else:
                    halos.append(jnp.where(own, turned(first, 64), last))

            def body(q, halos, group=group):
                index = jnp.where(lane < 96, (lane + 8 * q) & 63, 64 + ((lane + 8 + 8 * q) & 63))
                k = 8 * group + q
                for phase in range(4):
                    values = dense[which, phase // 2, k]
                    if phase % 2:
                        values = turned(values, 64)
                    target[phase, k] = jnp.where(own, values, picked(halos[phase], index))
                return halos

            lax.fori_loop(0, 8, body, tuple(halos), unroll=True)

    own_cells(1)
    counted = (
        (jnp.minimum(c, 2) + jnp.minimum(cross_count - 1 - c, 2) + 1) * (jnp.minimum(a, 1) + jnp.minimum(along_count - 1 - a, 1) + 1) - 1
    )
    pl.semaphore_wait(barrier, counted)
    density_copies = fine_copies(1)
    start(density_copies)
    own_cells(0)
    source_copies = fine_copies(0)
    start(source_copies)
    lane = lanes_of(FINE_ROWS)
    lane_16 = lanes_of(16)

    def pack(field, layer_of):
        near_index = 4 * (lane_16 & 15)
        far_index = 4 * ((lane_16 & 3) + 12 * (lane_16 >> 6))
        near_slot, far_slot = lane_16 >> 4, (lane_16 & 63) >> 2
        far = jnp.zeros((16, LANES), jnp.float32)
        for group in range(2):
            near = jnp.zeros((16, LANES), jnp.float32)
            for q in range(8):
                k = 8 * group + q
                value = layer_of(k)
                near = jnp.where(near_slot == q, value(near_index), near)
                far = jnp.where(far_slot == k, value(far_index), far)
            own_in[field, group, 0:16] = near
            near_out[0, field, group] = turned(near, 16)
            near_out[1, field, group] = turned(near, -16)
        low = lanes_of(8) < 64
        far_out[0, field] = jnp.where(low, far[0:8], turned(far[8:16], 64))
        far_out[1, field] = jnp.where(low, turned(far[0:8], 64), far[8:16])

    def own_upper(k):
        total = jnp.zeros((16, LANES), jnp.float32)
        for half in range(2):
            now = dense[1, half, k, 0:16]
            total += vertical_weight * harmonic(now, dense[1, half, k - 1, 0:16]) if k else 2.0 * vertical_weight * now
        total = paired_lanes(total + turned(total, 64), 1, lane_16)
        return lambda index: picked(total, index) + picked(total, index + 2)

    pack(2, own_upper)
    upper_copies = coarse_copies(0)
    start(upper_copies)
    for level in grid:
        level.close_upper()
    arrive(density_copies)
    whole_cells(1, cells)

    def faces(k, above):
        now = [cells[phase, k] for phase in range(4)]
        west, south, upper = [], [], []
        for phase in range(4):
            before = now[phase - 1] if phase else turned(now[3], 1)
            west.append(along_weight * harmonic(now[phase], row_turned(now[phase], 1)))
            south.append(cross_weight * harmonic(now[phase], before))
            upper.append(vertical_weight * harmonic(now[phase], above[phase]))
        upper = [jnp.where(k == 0, 2.0 * vertical_weight * now[phase], upper[phase]) for phase in range(4)]
        grid[0].set_faces(k, west, south, upper)
        west, south, upper = [west[0] + west[1], west[2] + west[3]], [0.5 * south[0], 0.5 * south[2]], [upper[0] + upper[1], upper[2] + upper[3]]
        grid[1].set_faces(k, west, south, upper)
        west, south, upper = [west[0] + west[1]], [0.5 * south[0]], [upper[0] + upper[1]]
        grid[2].set_faces(k, west, south, upper)
        west, south, upper = paired_lanes(west[0], 1, lane), 0.5 * first_child(south[0], 1, lane), paired_lanes(upper[0], 1, lane)
        grid[3].set_faces(k, [west], [south], [upper])
        return tuple(now)

    layers(faces, (jnp.ones((FINE_ROWS, LANES), jnp.float32),) * 4)

    def both(ref):
        def layer_of(k):
            values = ref[0, k, 0:16]
            return lambda index: picked(values, index) + picked(values, index + 2)

        return layer_of

    def half_first(ref):
        def layer_of(k):
            values = ref[0, k, 0:16]
            return lambda index: 0.5 * picked(values, index)

        return layer_of

    pack(0, both(grid[3].west))
    pack(1, half_first(grid[3].south))
    face_copies = coarse_copies(1)
    start(face_copies)

    factor(grid[:4], centre)

    arrive(source_copies)
    whole_cells(0, grid[0].forcing)

    def restrict(no):
        level, below = grid[no], grid[no + 1]

        def after(k, values):
            rest = level.remain(k, values)
            if level.phases > 1:
                for phase in range(below.phases):
                    below.forcing[phase, k] = rest[2 * phase] + rest[2 * phase + 1]
            else:
                below.forcing[0, k] = paired_lanes(rest[0], level.spread, lanes_of(level.rows))

        return after

    for no in (0, 1, 2):
        grid[no].start(held, restrict(no))
    third_copies = fresh_copies()
    start(third_copies)

    def keep_rest(k, values):
        cells[0, k] = grid[3].remain(k, values)[0]

    grid[3].start(held, keep_rest)
    pack(3, both(cells))
    forcing_copies = coarse_copies(2)
    start(forcing_copies)

    arrive(third_copies)

    def renew(k, _):
        grid[3].forcing[0, k, 16:24] = fresh[0, k]
        grid[3].forcing[0, k, 24:32] = fresh[1, k]
        return 0

    layers(renew, 0)
    grid[3].start(held, low=16)

    lane_8, lane_24 = lanes_of(8), lanes_of(COARSE_ROWS)
    low = lane_8 < 64

    def unpacked(field):
        fars = []
        for side in range(2):
            tiles = []
            for (low_no, low_half), (high_no, high_half) in (((2, 0), (0, 1)), ((2, 1), (1, 0)), ((0, 0), (1, 1))):
                lower, higher = far_in[side, low_no, field], far_in[side, high_no, field]
                lower = turned(lower, 64) if low_half else lower
                higher = higher if high_half else turned(higher, 64)
                tiles.append(jnp.where(low, lower, higher))
            fars.append(jnp.concatenate(tiles, 0))
        nears = []
        for group in range(2):
            for ref in (own_in.at[field, group], near_in.at[0, field, group], near_in.at[1, field, group]):
                nears.append((jnp.concatenate([ref[32:48], ref[0:8]], 0), turned(ref[8:32], 64)))
        slot, part = lane_24 >> 4, lane_24 & 63

        def layer_of(k):
            group, q = k // 8, k % 8
            own, after, before = nears[3 * group : 3 * group + 3]
            at = (slot - q) & 7
            mixed = own[0]
            for place, tile in ((1, after[0]), (7, before[0]), (4, own[1]), (5, after[1]), (3, before[1])):
                mixed = jnp.where(at == place, tile, mixed)
            mixed = turned(mixed, 24 - 16 * q)
            mixed = jnp.where(part >= 56, turned(fars[0], 56 - 4 * k), mixed)
            return jnp.where(part < 8, turned(fars[1], 4 - 4 * k), mixed)

        return layer_of

    arrive(upper_copies)
    arrive(face_copies)
    west_of, south_of, upper_of = unpacked(0), unpacked(1), unpacked(2)
    for k in range(NZ):
        west, south, upper = west_of(k), south_of(k), upper_of(k)
        grid[4].set_faces(k, [west], [south], [upper])
        for no in (5, 6):
            spread = grid[no].spread // 2
            west, south, upper = paired_lanes(west, spread, lane_24), 0.5 * first_child(south, spread, lane_24), paired_lanes(upper, spread, lane_24)
            grid[no].set_faces(k, [west], [south], [upper])
    factor(grid[4:])

    arrive(forcing_copies)
    forcing_of = unpacked(3)
    for k in range(NZ):
        grid[4].forcing[0, k] = forcing_of(k)

    grid[4].start(coarse_held, restrict(4))
    grid[5].start(coarse_held, restrict(5))
    grid[6].start(coarse_held)
    for _ in range(SWEEPS - 1):
        grid[6].sweep(coarse_held)
    grid[5].sweep(coarse_held, lambda k: [grid[6].value[0, k]])
    grid[4].sweep(coarse_held, lambda k: [grid[5].value[0, k]])

    row = lax.broadcasted_iota(jnp.int32, (FINE_ROWS, LANES), 0)
    third_index = jnp.where(lane < 96, (lane >> 2) + 24, (lane >> 2) - 8) + jnp.where((row >= 8) & (row < 24), 64, 0)

    def to_third(k):
        values = grid[4].value[0, k]
        return [picked(jnp.concatenate([values[16:24], values[0:16], values[8:16]], 0), third_index)]

    grid[3].sweep(held, to_third)
    grid[2].sweep(held, lambda k: [grid[3].value[0, k]])
    grid[1].sweep(held, lambda k: [grid[2].value[0, k]] * 2)
    grid[0].sweep(held, lambda k: [grid[1].value[phase // 2, k] for phase in range(4)])

    def laid_out(ref, k, phases):
        halves = [jnp.where(lane_16 < 64, phases[2 * half], turned(phases[2 * half + 1], 64)) for half in range(2)]
        index = (lane_16 & 1) * 64 + (lane_16 >> 2)
        for tile in range(2):
            at = index + 32 * tile
            raw[ref, k, :, tile * LANES : (tile + 1) * LANES] = jnp.where((lane_16 & 3) < 2, picked(halves[0], at), picked(halves[1], at))

    fine = grid[0]

    def finish(k, above):
        values = [fine.value[phase, k] for phase in range(4)]
        next_k = jnp.minimum(k + 1, NZ - 1)
        rest = []
        for phase, part in enumerate(fine.horizontal(k, values)):
            own = pl.ds(0, 16)
            below = fine.value[phase, next_k, own]
            rest.append(
                fine.forcing[phase, k, own]
                - (
                    centre[phase, k, own] * values[phase][0:16]
                    - part[0:16]
                    - fine.upper[phase, k, own] * above[phase]
                    - fine.upper[phase, k + 1, own] * below
                )
            )
        values = [value[0:16] for value in values]
        laid_out(0, k, values)
        laid_out(1, k, rest)
        return tuple(values)

    above = (jnp.zeros((16, LANES), jnp.float32),) * 4
    out_copies = []
    for part in range(2):
        done = pl.ds(8 * part, 8)
        above = lax.fori_loop(8 * part, 8 * part + 8, finish, above, unroll=True)
        for which, hbm in enumerate((pressure_hbm, residual_hbm)):
            out_copies.append(pltpu.make_async_copy(raw.at[which, done], hbm.at[done], out_sem.at[which, part]))
            out_copies[-1].start()

    for copies in (density_copies, source_copies, upper_copies, face_copies, third_copies, forcing_copies):
        leave(copies)
    for copy in out_copies:
        copy.wait()


def solution(mesh):
    cross_count, along_count = mesh.shape["cross"], mesh.shape["along"]

    def per_device(source, density):
        shape = jax.ShapeDtypeStruct(source.shape, jnp.float32)
        vmem = lambda *dims: pltpu.VMEM(dims, jnp.float32)
        scratch = [
            vmem(2, *source.shape),
            vmem(2, 2, NZ, FINE_ROWS, LANES),
            vmem(2, 2, 2, 16, LANES),
            vmem(2, 2, 2, 16, LANES),
            vmem(2, 2, 2, FINE_ROWS, LANES),
            vmem(2, 2, 2, FINE_ROWS, LANES),
            vmem(2, 4, 2, 16, LANES),
            vmem(2, 4, 8, LANES),
            vmem(4, 2, HELD_ROWS, LANES),
            vmem(2, 4, 2, HELD_ROWS, LANES),
            vmem(2, 3, 4, 8, LANES),
            vmem(2, NZ, 8, LANES),
            vmem(4, NZ, FINE_ROWS, LANES),
            vmem(4, NZ, FINE_ROWS, LANES),
            vmem(4, NZ, FINE_ROWS, LANES),
            vmem(1, NZ, COARSE_ROWS, LANES),
        ]
        for phases, rows in [(4, FINE_ROWS), (2, FINE_ROWS), (1, FINE_ROWS), (1, FINE_ROWS)] + [(1, COARSE_ROWS)] * 3:
            scratch += Level.scratch(phases, rows)
        scratch += [
            pltpu.SemaphoreType.DMA((2,)),
            pltpu.SemaphoreType.DMA((2, 2)),
            pltpu.SemaphoreType.DMA((2, len(FINE_SIDES))),
            pltpu.SemaphoreType.DMA((2, len(FINE_SIDES))),
            pltpu.SemaphoreType.DMA((3, len(COARSE_SIDES))),
            pltpu.SemaphoreType.DMA((3, len(COARSE_SIDES))),
            pltpu.SemaphoreType.DMA((2,)),
            pltpu.SemaphoreType.DMA((2,)),
        ]
        return pl.pallas_call(
            functools.partial(kernel, cross_count, along_count),
            out_shape=(shape, shape),
            in_specs=[pl.BlockSpec(memory_space=pl.ANY)] * 2,
            out_specs=(pl.BlockSpec(memory_space=pl.ANY),) * 2,
            scratch_shapes=scratch,
            compiler_params=pltpu.CompilerParams(collective_id=0, has_side_effects=True, vmem_limit_bytes=56 * 2**20),
        )(source, density)

    return jax.shard_map(
        per_device,
        mesh=mesh,
        in_specs=(P(None, "along", "cross"), P(None, "along", "cross")),
        out_specs=(P(None, "along", "cross"), P(None, "along", "cross")),
        check_vma=False,
    )
```

```python
import functools

import jax
import jax.numpy as jnp
from jax import lax
from jax.experimental import pallas as pl
from jax.experimental.pallas import tpu as pltpu
from jax.sharding import PartitionSpec as P

MESH = pl.DeviceIdType.MESH
SWEEPS = 4
NZ = 16
LANES = 128
FINE_ROWS = 32
COARSE_ROWS = 24
HELD_ROWS = 48
TINY = 1e-20

along_weight = 0.25
cross_weight = 1.0
vertical_weight = 0.5
relaxation = 0.8

COARSE_SIDES = [(d, e) for d in (1, -1, 2, -2, 0) for e in (0, 1, -1) if (d, e) != (0, 0)]
FINE_SIDES = [(d, e) for d in (1, -1, 0) for e in (0, 1, -1) if (d, e) != (0, 0)]


def layers(body, init, reverse=False):
    def step(i, carry):
        return body(NZ - 1 - i if reverse else i, carry)

    return lax.fori_loop(0, NZ, step, init, unroll=True)


def picked(values, lane_index):
    return jnp.take_along_axis(values, lane_index, axis=1, mode="promise_in_bounds")


def turned(values, by):
    return pltpu.roll(values, by % LANES, axis=1)


def row_turned(values, by):
    return pltpu.roll(values, by % values.shape[0], axis=0)


def harmonic(weight, first, second):
    product = first * second if weight == 0.5 else (2.0 * weight) * first * second
    return product * (1.0 / (first + second))


def lanes_of(rows):
    return lax.broadcasted_iota(jnp.int32, (rows, LANES), 1)


def row_before(values, folded):
    moved = row_turned(values, 1)
    if not folded:
        return moved
    head = moved[0:8]
    first = lax.broadcasted_iota(jnp.int32, head.shape, 0) == 0
    return jnp.concatenate([jnp.where(first, turned(head, 64), head), moved[8:]], 0)


def row_after(values, folded):
    moved = row_turned(values, -1)
    if not folded:
        return moved
    tail = moved[-8:]
    last = lax.broadcasted_iota(jnp.int32, tail.shape, 0) == 7
    return jnp.concatenate([moved[:-8], jnp.where(last, turned(tail, 64), tail)], 0)


class Level:
    def __init__(self, phases, spread, rows, refs):
        self.phases, self.spread, self.rows, self.folded = phases, spread, rows, rows == COARSE_ROWS
        self.west, self.south, self.upper, self.gain, self.pull, self.link, self.value, self.forcing = refs

    @staticmethod
    def scratch(phases, rows):
        full = pltpu.VMEM((phases, NZ, rows, LANES), jnp.float32)
        column = pltpu.VMEM((phases, NZ + 1, rows, LANES), jnp.float32)
        return [full, full, column, full, full, full, full, full]

    def horizontal(self, k, values):
        rows = pl.ds(0, values[0].shape[0])
        west = [self.west[phase, k, rows] for phase in range(self.phases)]
        south = [self.south[phase, k, rows] for phase in range(self.phases)]
        onward = [face * value for face, value in zip(south, values)]
        out = []
        for phase, value in enumerate(values):
            before = values[phase - 1] if phase else turned(values[-1], self.spread)
            north = onward[phase + 1] if phase + 1 < self.phases else turned(onward[0], -self.spread)
            along = west[phase] * row_before(value, self.folded) + row_after(west[phase] * value, self.folded)
            out.append(along + south[phase] * before + north)
        return out

    def set_faces(self, k, west, south, upper):
        for phase in range(self.phases):
            self.west[phase, k] = west[phase]
            self.south[phase, k] = south[phase]
            self.upper[phase, k] = upper[phase]

    def close_upper(self):
        for phase in range(self.phases):
            self.upper[phase, NZ] = jnp.zeros((self.rows, LANES), jnp.float32)

    def start(self, held, after=None, low=0):
        rows = pl.ds(low, self.rows - low)
        zero = jnp.zeros((self.rows - low, LANES), jnp.float32)

        def down(k, before):
            now = []
            for phase in range(self.phases):
                now.append(self.gain[phase, k, rows] * self.forcing[phase, k, rows] + self.pull[phase, k, rows] * before[phase])
                held[phase, k, rows] = now[-1]
            return tuple(now)

        layers(down, (zero,) * self.phases)

        def up(k, below):
            values = []
            for phase in range(self.phases):
                values.append(held[phase, k, rows] + self.link[phase, k, rows] * below[phase])
                self.value[phase, k, rows] = values[-1]
            if after is not None:
                after(k, values)
            return tuple(values)

        layers(up, (zero,) * self.phases, reverse=True)

    def remain(self, k, values):
        return [(1.0 - relaxation) * self.forcing[phase, k] + part for phase, part in enumerate(self.horizontal(k, values))]

    def near(self):
        first = lax.broadcasted_iota(jnp.int32, (8, LANES), 0) < 4

        def body(k, _):
            for ref in (self.west, self.south, self.gain, self.pull, self.link, self.value, self.forcing):
                for phase in range(self.phases):
                    ref[phase, k, 16:24] = jnp.where(first, ref[phase, k, 16:24], ref[phase, k, 24:32])
            return 0

        layers(body, 0)
        self.rows = 24

    def sweep(self, held, coarse=None, after=None):
        zero = jnp.zeros((self.rows, LANES), jnp.float32)
        rows = pl.ds(0, self.rows)

        def down(k, before):
            values = [self.value[phase, k, rows] for phase in range(self.phases)]
            if coarse is not None:
                values = [value + extra for value, extra in zip(values, coarse(k))]
                for phase in range(self.phases):
                    self.value[phase, k, rows] = values[phase]
            now = []
            for phase, part in enumerate(self.horizontal(k, values)):
                now.append(self.gain[phase, k, rows] * (self.forcing[phase, k, rows] + part) + self.pull[phase, k, rows] * before[phase])
                held[phase, k, rows] = now[-1]
            return tuple(now)

        layers(down, (zero,) * self.phases)

        def up(k, below):
            now, values = [], []
            for phase in range(self.phases):
                now.append(held[phase, k, rows] + self.link[phase, k, rows] * below[phase])
                values.append((1.0 - relaxation) * self.value[phase, k, rows] + now[-1])
                self.value[phase, k, rows] = values[-1]
            if after is not None:
                after(k, values)
            return tuple(now)

        layers(up, (zero,) * self.phases, reverse=True)


def factor(levels, centre_ref=None):
    def body(k, before):
        now = []
        for no, level in enumerate(levels):
            links = []
            for phase in range(level.phases):
                upper, lower = level.upper[phase, k], level.upper[phase, k + 1]
                west, south = level.west[phase, k], level.south[phase, k]
                north = level.south[phase + 1, k] if phase + 1 < level.phases else turned(level.south[0, k], -level.spread)
                centre = west + row_after(west, level.folded) + south + north + upper + lower
                if no == 0 and centre_ref is not None:
                    centre_ref[phase, k] = centre
                inverse = 1.0 / jnp.maximum(centre - upper * before[no][phase], TINY)
                level.gain[phase, k] = relaxation * inverse
                level.pull[phase, k] = upper * inverse
                links.append(lower * inverse)
                level.link[phase, k] = links[-1]
            now.append(tuple(links))
        return tuple(now)

    layers(body, tuple((jnp.zeros((level.rows, LANES), jnp.float32),) * level.phases for level in levels))


def paired_lanes(values, spread):
    return values + turned(values, -spread)


def both_children(values, spread, lane):
    return jnp.where((lane & spread) == 0, values, turned(values, spread))


def kernel(
    cross_count,
    along_count,
    source_hbm,
    density_hbm,
    pressure_hbm,
    residual_hbm,
    raw,
    dense,
    first_out,
    last_out,
    first_in,
    last_in,
    near_out,
    far_out,
    own_in,
    near_in,
    far_in,
    fresh,
    cells,
    centre,
    held,
    coarse_held,
    *rest,
):
    level_refs, (own_sem, out_sem, fine_send, fine_recv, coarse_send, coarse_recv, fresh_send, fresh_recv) = rest[:-8], rest[-8:]
    shapes = [(4, 1, FINE_ROWS), (2, 1, FINE_ROWS), (1, 1, FINE_ROWS), (1, 2, FINE_ROWS), (1, 1, COARSE_ROWS), (1, 2, COARSE_ROWS), (1, 4, COARSE_ROWS)]
    grid = [Level(*shape, level_refs[8 * no : 8 * no + 8]) for no, shape in enumerate(shapes)]
    c, a = lax.axis_index("cross"), lax.axis_index("along")

    def inside(d, e):
        return (c + d >= 0) & (c + d < cross_count) & (a + e >= 0) & (a + e < along_count)

    own_copies = [pltpu.make_async_copy(hbm, raw.at[which], own_sem.at[which]) for which, hbm in ((0, source_hbm), (1, density_hbm))]
    for copy in own_copies[::-1]:
        copy.start()

    for ref in (own_in, near_in, far_in, fresh):
        ref[...] = jnp.zeros(ref.shape, ref.dtype)
    dense[0, :, :, 16:32, :] = jnp.zeros((2, NZ, 16, LANES), jnp.float32)
    dense[1, :, :, 16:32, :] = jnp.full((2, NZ, 16, LANES), TINY, jnp.float32)
    for ref in (first_in, last_in):
        ref[0] = jnp.zeros(ref.shape[1:], ref.dtype)
        ref[1] = jnp.full(ref.shape[1:], TINY, ref.dtype)

    barrier = pltpu.get_barrier_semaphore()
    for d, e in COARSE_SIDES:

        @pl.when(inside(d, e))
        def _(d=d, e=e):
            pl.semaphore_signal(barrier, inc=1, device_id=(c + d, a + e), device_id_type=MESH)

    def own_cells(which, target):
        own_copies[which].wait()
        ref = raw.at[which]
        lane = lanes_of(16)
        index = (4 * (lane & 63) + (lane >> 6)) & 127
        lower = (lane & 63) < 32

        def body(k, _):
            left, right = ref[k, :, 0:LANES], ref[k, :, LANES : 2 * LANES]
            for half in range(2):
                at = index + 2 * half
                values = jnp.where(lower, picked(left, at), picked(right, at))
                dense[which, half, k, 0:16] = values
                target[2 * half, k, 0:16] = values
                target[2 * half + 1, k, 0:16] = turned(values, 64)
            return 0

        layers(body, 0)
        part = lane & 63
        for half in range(2):
            for group in range(2):
                first = last = jnp.zeros((16, LANES), jnp.float32)
                for q in range(8):
                    values = dense[which, half, 8 * group + q, 0:16]
                    here = (part >= 7 * q) & (part < 7 * q + 7)
                    first = jnp.where(here, turned(values, 7 * q), first)
                    last = jnp.where(here, turned(values, 7 * q - 58), last)
                first_out[which, half, group] = first
                last_out[which, half, group] = last

    def fine_copies(which):
        copies = []
        for no, (d, e) in enumerate(FINE_SIDES):
            rows_from = {0: (0, 16), 1: (0, 8), -1: (8, 16)}[e]
            rows_to = {0: (0, 16), 1: (16, 24), -1: (24, 32)}[e]
            take, put = pl.ds(rows_from[0], rows_from[1] - rows_from[0]), pl.ds(rows_to[0], rows_to[1] - rows_to[0])
            if d == 0:
                src, dst = dense.at[which, :, :, take, :], dense.at[which, :, :, put, :]
            elif d == 1:
                src, dst = first_out.at[which, :, :, take, :], first_in.at[which, :, :, put, :]
            else:
                src, dst = last_out.at[which, :, :, take, :], last_in.at[which, :, :, put, :]
            copies.append(
                (
                    d,
                    e,
                    pltpu.make_async_remote_copy(
                        src_ref=src,
                        dst_ref=dst,
                        send_sem=fine_send.at[which, no],
                        recv_sem=fine_recv.at[which, no],
                        device_id=(c - d, a - e),
                        device_id_type=MESH,
                    ),
                )
            )
        return copies

    def coarse_copies(which):
        fields = (pl.ds(2, 1), pl.ds(0, 2), pl.ds(3, 1))[which]
        copies = []
        for no, (d, e) in enumerate(COARSE_SIDES):
            put = pl.ds({0: 0, 1: 16, -1: 32}[e], 16)
            if d == 0:
                src, dst = own_in.at[fields, :, pl.ds(0, 16), :], own_in.at[fields, :, put, :]
            elif abs(d) == 1:
                side = 0 if d > 0 else 1
                src, dst = near_out.at[side, fields], near_in.at[side, fields, :, put, :]
            else:
                side = 0 if d > 0 else 1
                src, dst = far_out.at[side, fields], far_in.at[side, {0: 0, 1: 1, -1: 2}[e], fields]
            copies.append(
                (
                    d,
                    e,
                    pltpu.make_async_remote_copy(
                        src_ref=src,
                        dst_ref=dst,
                        send_sem=coarse_send.at[which, no],
                        recv_sem=coarse_recv.at[which, no],
                        device_id=(c - d, a - e),
                        device_id_type=MESH,
                    ),
                )
            )
        return copies

    def fresh_copies():
        copies = []
        for no, (e, take) in enumerate([(1, 0), (-1, 8)]):
            copies.append(
                (
                    0,
                    e,
                    pltpu.make_async_remote_copy(
                        src_ref=grid[3].forcing.at[0, :, pl.ds(take, 8), :],
                        dst_ref=fresh.at[no],
                        send_sem=fresh_send.at[no],
                        recv_sem=fresh_recv.at[no],
                        device_id=(c, a - e),
                        device_id_type=MESH,
                    ),
                )
            )
        return copies

    def start(copies):
        for d, e, copy in copies:
            pl.when(inside(-d, -e))(copy.start)

    def arrive(copies):
        for d, e, copy in copies:
            pl.when(inside(d, e))(copy.wait_recv)

    def leave(copies):
        for d, e, copy in copies:
            pl.when(inside(-d, -e))(copy.wait_send)

    def whole_cells(which, target):
        lane = lanes_of(FINE_ROWS)
        own = lanes_of(16) < 64
        for group in range(2):
            halos = []
            for phase in range(4):
                first, last = first_in[which, phase // 2, group], last_in[which, phase // 2, group]
                if phase % 2 == 0:
                    halos.append(jnp.where(lane < 56, first, turned(last, 58)))
                else:
                    halos.append(jnp.where(lane < 56, turned(first, 64), turned(last, -6)))
            for q in range(8):
                k = 8 * group + q
                for phase in range(4):
                    edges = turned(halos[phase], 64 - 7 * q)
                    values = dense[which, phase // 2, k, 16:32]
                    values = turned(values, 64) if phase % 2 else values
                    target[phase, k, 0:16] = jnp.where(own, target[phase, k, 0:16], edges[0:16])
                    target[phase, k, 16:32] = jnp.where(own, values, edges[16:32])

    own_cells(1, cells)
    counted = (
        (jnp.minimum(c, 2) + jnp.minimum(cross_count - 1 - c, 2) + 1) * (jnp.minimum(a, 1) + jnp.minimum(along_count - 1 - a, 1) + 1) - 1
    )
    pl.semaphore_wait(barrier, counted)
    density_copies = fine_copies(1)
    start(density_copies)
    own_cells(0, grid[0].forcing)
    source_copies = fine_copies(0)
    start(source_copies)
    lane = lanes_of(FINE_ROWS)
    lane_16 = lanes_of(16)

    def pack(field, layer_of):
        near_index = 4 * (lane_16 & 15)
        far_index = 16 * ((lane_16 >> 2) & 7) + (lane_16 & 3) + 12 * (lane_16 >> 6)
        slot = lane_16 >> 4
        fars = []
        for group in range(2):
            near = jnp.zeros((16, LANES), jnp.float32)
            for q in range(8):
                near = jnp.where(slot == q, picked(layer_of(8 * group + q), near_index), near)
            own_in[field, group, 0:16] = near
            near_out[0, field, group] = turned(near, 16)
            near_out[1, field, group] = turned(near, -16)
            fars.append(picked(near, far_index))
        far = jnp.where((lane_16 & 63) < 32, fars[0], fars[1])
        low = lanes_of(8) < 64
        far_out[0, field] = jnp.where(low, far[0:8], turned(far[8:16], 64))
        far_out[1, field] = jnp.where(low, turned(far[0:8], 64), far[8:16])

    def own_upper(k):
        total = jnp.zeros((16, LANES), jnp.float32)
        for half in range(2):
            now = dense[1, half, k, 0:16]
            total += harmonic(vertical_weight, now, dense[1, half, k - 1, 0:16]) if k else 2.0 * vertical_weight * now
        return paired_lanes(paired_lanes(total + turned(total, 64), 1), 2)

    pack(2, own_upper)
    upper_copies = coarse_copies(0)
    start(upper_copies)
    for level in grid:
        level.close_upper()
    arrive(density_copies)
    whole_cells(1, cells)

    def faces(k, above):
        now = [cells[phase, k] for phase in range(4)]
        west, south, upper = [], [], []
        for phase in range(4):
            before = now[phase - 1] if phase else turned(now[3], 1)
            west.append(harmonic(along_weight, now[phase], row_turned(now[phase], 1)))
            south.append(harmonic(cross_weight, now[phase], before))
            upper.append(harmonic(vertical_weight, now[phase], above[phase]))
        upper = [jnp.where(k == 0, 2.0 * vertical_weight * now[phase], upper[phase]) for phase in range(4)]
        grid[0].set_faces(k, west, south, upper)
        west, south, upper = [west[0] + west[1], west[2] + west[3]], [0.5 * south[0], 0.5 * south[2]], [upper[0] + upper[1], upper[2] + upper[3]]
        grid[1].set_faces(k, west, south, upper)
        west, south, upper = [west[0] + west[1]], [0.5 * south[0]], [upper[0] + upper[1]]
        grid[2].set_faces(k, west, south, upper)
        west, south, upper = paired_lanes(west[0], 1), 0.5 * south[0], paired_lanes(upper[0], 1)
        grid[3].set_faces(k, [west], [south], [upper])
        return tuple(now)

    layers(faces, (jnp.ones((FINE_ROWS, LANES), jnp.float32),) * 4)

    pack(0, lambda k: paired_lanes(grid[3].west[0, k, 0:16], 2))
    pack(1, lambda k: 0.5 * grid[3].south[0, k, 0:16])
    face_copies = coarse_copies(1)
    start(face_copies)

    factor(grid[:4], centre)

    arrive(source_copies)
    whole_cells(0, grid[0].forcing)

    def restrict(no):
        level, below = grid[no], grid[no + 1]

        def after(k, values):
            rest = level.remain(k, values)
            if level.phases > 1:
                for phase in range(below.phases):
                    below.forcing[phase, k] = rest[2 * phase] + rest[2 * phase + 1]
            else:
                below.forcing[0, k] = paired_lanes(rest[0], level.spread)

        return after

    for no in (0, 1, 2):
        grid[no].start(held, restrict(no))
    third_copies = fresh_copies()
    start(third_copies)

    def keep_rest(k, values):
        cells[0, k] = grid[3].remain(k, values)[0]

    grid[3].start(held, keep_rest)
    pack(3, lambda k: paired_lanes(cells[0, k, 0:16], 2))
    forcing_copies = coarse_copies(2)
    start(forcing_copies)

    arrive(third_copies)

    def renew(k, _):
        grid[3].forcing[0, k, 16:24] = fresh[0, k]
        grid[3].forcing[0, k, 24:32] = fresh[1, k]
        return 0

    layers(renew, 0)
    grid[3].start(held, low=16)

    lane_8, lane_24 = lanes_of(8), lanes_of(COARSE_ROWS)

    def unpacked(field):
        slot_8, part_8, inner = lane_8 >> 4, lane_8 & 3, (lane_8 & 15) < 8

        def far(side, no, half, group, shift):
            return picked(far_in[side, no, field], 64 * half + 4 * (8 * group + ((slot_8 - shift) & 7)) + part_8)

        tiles = [((2, 0), (0, 1)), ((2, 1), (1, 0)), ((0, 0), (1, 1))]
        sources = []
        for group in range(2):
            places = {}
            for place, ref in ((0, own_in.at[field, group]), (1, near_in.at[0, field, group]), (7, near_in.at[1, field, group])):
                places[place] = jnp.concatenate([ref[32:48], ref[0:8]], 0)
                places[(place + 4) % 8] = turned(ref[8:32], 64)
            places[2] = jnp.concatenate([jnp.where(inner, far(0, *lower, group, 2), far(1, *higher, group, 2)) for lower, higher in tiles], 0)
            places[6] = jnp.concatenate([jnp.where(inner, far(0, *higher, group, 6), far(1, *lower, group, 6)) for lower, higher in tiles], 0)
            sources.append(places)
        slot = lane_24 >> 4

        def layer_of(k):
            places, q = sources[k // 8], k % 8
            at = (slot - q) & 7
            mixed = places[0]
            for place in range(1, 8):
                mixed = jnp.where(at == place, places[place], mixed)
            return turned(mixed, 24 - 16 * q)

        return layer_of

    arrive(upper_copies)
    arrive(face_copies)
    west_of, south_of, upper_of = unpacked(0), unpacked(1), unpacked(2)
    for k in range(NZ):
        west, south, upper = west_of(k), south_of(k), upper_of(k)
        grid[4].set_faces(k, [west], [south], [upper])
        for no in (5, 6):
            spread = grid[no].spread // 2
            west, south, upper = paired_lanes(west, spread), 0.5 * south, paired_lanes(upper, spread)
            grid[no].set_faces(k, [west], [south], [upper])
    factor(grid[4:])
    for level in grid[:3]:
        level.near()

    arrive(forcing_copies)
    forcing_of = unpacked(3)
    for k in range(NZ):
        grid[4].forcing[0, k] = forcing_of(k)

    grid[4].start(coarse_held, restrict(4))
    grid[5].start(coarse_held, restrict(5))
    grid[6].start(coarse_held)
    for _ in range(SWEEPS - 1):
        grid[6].sweep(coarse_held)
    grid[5].sweep(coarse_held, lambda k: [both_children(grid[6].value[0, k], 2, lane_24)])
    grid[4].sweep(coarse_held, lambda k: [both_children(grid[5].value[0, k], 1, lane_24)])

    row = lax.broadcasted_iota(jnp.int32, (FINE_ROWS, LANES), 0)
    third_index = jnp.where(lane < 96, (lane >> 2) + 24, (lane >> 2) - 8) + jnp.where((row >= 8) & (row < 24), 64, 0)

    def to_third(k):
        values = grid[4].value[0, k]
        return [picked(jnp.concatenate([values[16:24], values[0:16], values[8:16]], 0), third_index)]

    grid[3].sweep(held, to_third)
    first = lax.broadcasted_iota(jnp.int32, (8, LANES), 0) < 4

    def to_second(k):
        values = grid[3].value[0, k]
        values = jnp.concatenate([values[0:16], jnp.where(first, values[16:24], values[24:32])], 0)
        return [both_children(values, 1, lane_24)]

    grid[2].sweep(held, to_second)
    grid[1].sweep(held, lambda k: [grid[2].value[0, k, 0:24]] * 2)
    def laid_out(ref, k, phases):
        halves = [jnp.where(lane_16 < 64, phases[2 * half], turned(phases[2 * half + 1], 64)) for half in range(2)]
        index = (lane_16 & 1) * 64 + (lane_16 >> 2)
        for tile in range(2):
            at = index + 32 * tile
            raw[ref, k, :, tile * LANES : (tile + 1) * LANES] = jnp.where((lane_16 & 3) < 2, picked(halves[0], at), picked(halves[1], at))

    fine = grid[0]
    grid[0].sweep(held, lambda k: [grid[1].value[phase // 2, k, 0:24] for phase in range(4)], lambda k, values: laid_out(0, k, [value[0:16] for value in values]))
    out_copies = [pltpu.make_async_copy(raw.at[0], pressure_hbm, out_sem.at[0, 0])]
    out_copies[0].start()

    def finish(k, above):
        values = [fine.value[phase, k, 0:24] for phase in range(4)]
        next_k = jnp.minimum(k + 1, NZ - 1)
        rest = []
        for phase, part in enumerate(fine.horizontal(k, values)):
            own = pl.ds(0, 16)
            below = fine.value[phase, next_k, own]
            rest.append(
                fine.forcing[phase, k, own]
                - (
                    centre[phase, k, own] * values[phase][0:16]
                    - part[0:16]
                    - fine.upper[phase, k, own] * above[phase]
                    - fine.upper[phase, k + 1, own] * below
                )
            )
        values = [value[0:16] for value in values]
        laid_out(1, k, rest)
        return tuple(values)

    above = (jnp.zeros((16, LANES), jnp.float32),) * 4
    for part in range(2):
        done = pl.ds(8 * part, 8)
        above = lax.fori_loop(8 * part, 8 * part + 8, finish, above, unroll=True)
        out_copies.append(pltpu.make_async_copy(raw.at[1, done], residual_hbm.at[done], out_sem.at[1, part]))
        out_copies[-1].start()

    for copies in (density_copies, source_copies, upper_copies, face_copies, third_copies, forcing_copies):
        leave(copies)
    for copy in out_copies:
        copy.wait()


def hand_on(pressure_in, residual_in, pressure_out, residual_out):
    pressure_out[...] = pressure_in[...]
    residual_out[...] = residual_in[...]


def solution(mesh):
    cross_count, along_count = mesh.shape["cross"], mesh.shape["along"]

    def per_device(source, density):
        shape = jax.ShapeDtypeStruct(source.shape, jnp.float32)
        vmem = lambda *dims: pltpu.VMEM(dims, jnp.float32)
        scratch = [
            vmem(2, *source.shape),
            vmem(2, 2, NZ, FINE_ROWS, LANES),
            vmem(2, 2, 2, 16, LANES),
            vmem(2, 2, 2, 16, LANES),
            vmem(2, 2, 2, FINE_ROWS, LANES),
            vmem(2, 2, 2, FINE_ROWS, LANES),
            vmem(2, 4, 2, 16, LANES),
            vmem(2, 4, 8, LANES),
            vmem(4, 2, HELD_ROWS, LANES),
            vmem(2, 4, 2, HELD_ROWS, LANES),
            vmem(2, 3, 4, 8, LANES),
            vmem(2, NZ, 8, LANES),
            vmem(4, NZ, FINE_ROWS, LANES),
            vmem(4, NZ, FINE_ROWS, LANES),
            vmem(4, NZ, FINE_ROWS, LANES),
            vmem(1, NZ, COARSE_ROWS, LANES),
        ]
        for phases, rows in [(4, FINE_ROWS), (2, FINE_ROWS), (1, FINE_ROWS), (1, FINE_ROWS)] + [(1, COARSE_ROWS)] * 3:
            scratch += Level.scratch(phases, rows)
        scratch += [
            pltpu.SemaphoreType.DMA((2,)),
            pltpu.SemaphoreType.DMA((2, 2)),
            pltpu.SemaphoreType.DMA((2, len(FINE_SIDES))),
            pltpu.SemaphoreType.DMA((2, len(FINE_SIDES))),
            pltpu.SemaphoreType.DMA((3, len(COARSE_SIDES))),
            pltpu.SemaphoreType.DMA((3, len(COARSE_SIDES))),
            pltpu.SemaphoreType.DMA((2,)),
            pltpu.SemaphoreType.DMA((2,)),
        ]
        pressure, residual = pl.pallas_call(
            functools.partial(kernel, cross_count, along_count),
            out_shape=(shape, shape),
            in_specs=[pl.BlockSpec(memory_space=pl.ANY)] * 2,
            out_specs=(pl.BlockSpec(memory_space=pl.ANY),) * 2,
            scratch_shapes=scratch,
            compiler_params=pltpu.CompilerParams(collective_id=0, has_side_effects=True, vmem_limit_bytes=56 * 2**20),
        )(source, density)
        return pl.pallas_call(
            hand_on,
            out_shape=(shape, shape),
            in_specs=[pl.BlockSpec(memory_space=pltpu.VMEM)] * 2,
            out_specs=(pl.BlockSpec(memory_space=pltpu.VMEM),) * 2,
        )(pressure, residual)

    return jax.shard_map(
        per_device,
        mesh=mesh,
        in_specs=(P(None, "along", "cross"), P(None, "along", "cross")),
        out_specs=(P(None, "along", "cross"), P(None, "along", "cross")),
        check_vma=False,
    )
```

```python
import functools

import jax
import jax.numpy as jnp
from jax import lax
from jax.experimental import pallas as pl
from jax.experimental.pallas import tpu as pltpu
from jax.sharding import PartitionSpec as P

MESH = pl.DeviceIdType.MESH
SWEEPS = 4
NZ = 16
LANES = 128
FINE_ROWS = 32
COARSE_ROWS = 24
HELD_ROWS = 48
TINY = 1e-20

along_weight = 0.25
cross_weight = 1.0
vertical_weight = 0.5
relaxation = 0.8

COARSE_SIDES = [(d, e) for d in (1, -1, 2, -2, 0) for e in (0, 1, -1) if (d, e) != (0, 0)]
FINE_SIDES = [(d, e) for d in (1, -1, 0) for e in (0, 1, -1) if (d, e) != (0, 0)]


def layers(body, init, reverse=False):
    def step(i, carry):
        return body(NZ - 1 - i if reverse else i, carry)

    return lax.fori_loop(0, NZ, step, init, unroll=True)


def picked(values, lane_index):
    return jnp.take_along_axis(values, lane_index, axis=1, mode="promise_in_bounds")


def turned(values, by):
    return pltpu.roll(values, by % LANES, axis=1)


def row_turned(values, by):
    return pltpu.roll(values, by % values.shape[0], axis=0)


def harmonic(weight, first, second):
    product = first * second if weight == 0.5 else (2.0 * weight) * first * second
    return product * (1.0 / (first + second))


def lanes_of(rows):
    return lax.broadcasted_iota(jnp.int32, (rows, LANES), 1)


def row_before(values, folded):
    moved = row_turned(values, 1)
    if not folded:
        return moved
    head = moved[0:8]
    first = lax.broadcasted_iota(jnp.int32, head.shape, 0) == 0
    return jnp.concatenate([jnp.where(first, turned(head, 64), head), moved[8:]], 0)


def row_after(values, folded):
    moved = row_turned(values, -1)
    if not folded:
        return moved
    tail = moved[-8:]
    last = lax.broadcasted_iota(jnp.int32, tail.shape, 0) == 7
    return jnp.concatenate([moved[:-8], jnp.where(last, turned(tail, 64), tail)], 0)


class Level:
    def __init__(self, phases, spread, rows, refs):
        self.phases, self.spread, self.rows, self.folded = phases, spread, rows, rows == COARSE_ROWS
        self.west, self.south, self.upper, self.gain, self.pull, self.link, self.value, self.forcing = refs

    @staticmethod
    def scratch(phases, rows):
        full = pltpu.VMEM((phases, NZ, rows, LANES), jnp.float32)
        column = pltpu.VMEM((phases, NZ + 1, rows, LANES), jnp.float32)
        return [full, full, column, full, full, full, full, full]

    def horizontal(self, k, values):
        rows = pl.ds(0, values[0].shape[0])
        west = [self.west[phase, k, rows] for phase in range(self.phases)]
        south = [self.south[phase, k, rows] for phase in range(self.phases)]
        onward = [face * value for face, value in zip(south, values)]
        out = []
        for phase, value in enumerate(values):
            before = values[phase - 1] if phase else turned(values[-1], self.spread)
            north = onward[phase + 1] if phase + 1 < self.phases else turned(onward[0], -self.spread)
            along = west[phase] * row_before(value, self.folded) + row_after(west[phase] * value, self.folded)
            out.append(along + south[phase] * before + north)
        return out

    def set_faces(self, k, west, south, upper):
        for phase in range(self.phases):
            self.west[phase, k] = west[phase]
            self.south[phase, k] = south[phase]
            self.upper[phase, k] = upper[phase]

    def close_upper(self):
        for phase in range(self.phases):
            self.upper[phase, NZ] = jnp.zeros((self.rows, LANES), jnp.float32)

    def start(self, held, after=None, low=0):
        rows = pl.ds(low, self.rows - low)
        zero = jnp.zeros((self.rows - low, LANES), jnp.float32)

        def down(k, before):
            now = []
            for phase in range(self.phases):
                now.append(self.gain[phase, k, rows] * self.forcing[phase, k, rows] + self.pull[phase, k, rows] * before[phase])
                held[phase, k, rows] = now[-1]
            return tuple(now)

        layers(down, (zero,) * self.phases)

        def up(k, below):
            values = []
            for phase in range(self.phases):
                values.append(held[phase, k, rows] + self.link[phase, k, rows] * below[phase])
                self.value[phase, k, rows] = values[-1]
            if after is not None:
                after(k, values)
            return tuple(values)

        layers(up, (zero,) * self.phases, reverse=True)

    def remain(self, k, values):
        return [(1.0 - relaxation) * self.forcing[phase, k] + part for phase, part in enumerate(self.horizontal(k, values))]

    def near(self):
        first = lax.broadcasted_iota(jnp.int32, (8, LANES), 0) < 4

        def body(k, _):
            for ref in (self.west, self.south, self.gain, self.pull, self.link, self.value, self.forcing):
                for phase in range(self.phases):
                    ref[phase, k, 16:24] = jnp.where(first, ref[phase, k, 16:24], ref[phase, k, 24:32])
            return 0

        layers(body, 0)
        self.rows = 24

    def sweep(self, held, coarse=None, after=None):
        zero = jnp.zeros((self.rows, LANES), jnp.float32)
        rows = pl.ds(0, self.rows)

        def down(k, before):
            values = [self.value[phase, k, rows] for phase in range(self.phases)]
            if coarse is not None:
                values = [value + extra for value, extra in zip(values, coarse(k))]
                for phase in range(self.phases):
                    self.value[phase, k, rows] = values[phase]
            now = []
            for phase, part in enumerate(self.horizontal(k, values)):
                now.append(self.gain[phase, k, rows] * (self.forcing[phase, k, rows] + part) + self.pull[phase, k, rows] * before[phase])
                held[phase, k, rows] = now[-1]
            return tuple(now)

        layers(down, (zero,) * self.phases)

        def up(k, below):
            now, values = [], []
            for phase in range(self.phases):
                now.append(held[phase, k, rows] + self.link[phase, k, rows] * below[phase])
                values.append((1.0 - relaxation) * self.value[phase, k, rows] + now[-1])
                self.value[phase, k, rows] = values[-1]
            if after is not None:
                after(k, values)
            return tuple(now)

        layers(up, (zero,) * self.phases, reverse=True)


def factor(levels, centre_ref=None):
    def body(k, before):
        now = []
        for no, level in enumerate(levels):
            links = []
            for phase in range(level.phases):
                upper, lower = level.upper[phase, k], level.upper[phase, k + 1]
                west, south = level.west[phase, k], level.south[phase, k]
                north = level.south[phase + 1, k] if phase + 1 < level.phases else turned(level.south[0, k], -level.spread)
                centre = west + row_after(west, level.folded) + south + north + upper + lower
                if no == 0 and centre_ref is not None:
                    centre_ref[phase, k] = centre
                inverse = 1.0 / jnp.maximum(centre - upper * before[no][phase], TINY)
                level.gain[phase, k] = relaxation * inverse
                level.pull[phase, k] = upper * inverse
                links.append(lower * inverse)
                level.link[phase, k] = links[-1]
            now.append(tuple(links))
        return tuple(now)

    layers(body, tuple((jnp.zeros((level.rows, LANES), jnp.float32),) * level.phases for level in levels))


def paired_lanes(values, spread):
    return values + turned(values, -spread)


def both_children(values, spread, lane):
    return jnp.where((lane & spread) == 0, values, turned(values, spread))


def kernel(
    cross_count,
    along_count,
    source_hbm,
    density_hbm,
    pressure_ref,
    residual_ref,
    raw,
    dense,
    first_out,
    last_out,
    first_in,
    last_in,
    near_out,
    far_out,
    own_in,
    near_in,
    far_in,
    fresh,
    cells,
    centre,
    held,
    coarse_held,
    *rest,
):
    level_refs, (own_sem, fine_send, fine_recv, coarse_send, coarse_recv, fresh_send, fresh_recv) = rest[:-7], rest[-7:]
    shapes = [(4, 1, FINE_ROWS), (2, 1, FINE_ROWS), (1, 1, FINE_ROWS), (1, 2, FINE_ROWS), (1, 1, COARSE_ROWS), (1, 2, COARSE_ROWS), (1, 4, COARSE_ROWS)]
    grid = [Level(*shape, level_refs[8 * no : 8 * no + 8]) for no, shape in enumerate(shapes)]
    c, a = lax.axis_index("cross"), lax.axis_index("along")

    def inside(d, e):
        return (c + d >= 0) & (c + d < cross_count) & (a + e >= 0) & (a + e < along_count)

    own_copies = [pltpu.make_async_copy(hbm, raw.at[which], own_sem.at[which]) for which, hbm in ((0, source_hbm), (1, density_hbm))]
    for copy in own_copies[::-1]:
        copy.start()

    @pl.when((c < 2) | (c > cross_count - 3) | (a < 1) | (a > along_count - 2))
    def _():
        for ref in (own_in, near_in, far_in, fresh):
            ref[...] = jnp.zeros(ref.shape, ref.dtype)
        dense[0, :, :, 16:32, :] = jnp.zeros((2, NZ, 16, LANES), jnp.float32)
        dense[1, :, :, 16:32, :] = jnp.full((2, NZ, 16, LANES), TINY, jnp.float32)
        for ref in (first_in, last_in):
            ref[0] = jnp.zeros(ref.shape[1:], ref.dtype)
            ref[1] = jnp.full(ref.shape[1:], TINY, ref.dtype)

    barrier = pltpu.get_barrier_semaphore()
    for d, e in COARSE_SIDES:

        @pl.when(inside(d, e))
        def _(d=d, e=e):
            pl.semaphore_signal(barrier, inc=1, device_id=(c + d, a + e), device_id_type=MESH)

    def own_cells(which, target):
        own_copies[which].wait()
        ref = raw.at[which]
        lane = lanes_of(16)
        index = (4 * (lane & 63) + (lane >> 6)) & 127
        lower = (lane & 63) < 32

        def body(k, _):
            left, right = ref[k, :, 0:LANES], ref[k, :, LANES : 2 * LANES]
            for half in range(2):
                at = index + 2 * half
                values = jnp.where(lower, picked(left, at), picked(right, at))
                dense[which, half, k, 0:16] = values
                target[2 * half, k, 0:16] = values
                target[2 * half + 1, k, 0:16] = turned(values, 64)
            return 0

        layers(body, 0)
        part = lane & 63
        for half in range(2):
            for group in range(2):
                first = last = jnp.zeros((16, LANES), jnp.float32)
                for q in range(8):
                    values = dense[which, half, 8 * group + q, 0:16]
                    here = (part >= 7 * q) & (part < 7 * q + 7)
                    first = jnp.where(here, turned(values, 7 * q), first)
                    last = jnp.where(here, turned(values, 7 * q - 58), last)
                first_out[which, half, group] = first
                last_out[which, half, group] = last

    def fine_copies(which):
        copies = []
        for no, (d, e) in enumerate(FINE_SIDES):
            rows_from = {0: (0, 16), 1: (0, 8), -1: (8, 16)}[e]
            rows_to = {0: (0, 16), 1: (16, 24), -1: (24, 32)}[e]
            take, put = pl.ds(rows_from[0], rows_from[1] - rows_from[0]), pl.ds(rows_to[0], rows_to[1] - rows_to[0])
            if d == 0:
                src, dst = dense.at[which, :, :, take, :], dense.at[which, :, :, put, :]
            elif d == 1:
                src, dst = first_out.at[which, :, :, take, :], first_in.at[which, :, :, put, :]
            else:
                src, dst = last_out.at[which, :, :, take, :], last_in.at[which, :, :, put, :]
            copies.append(
                (
                    d,
                    e,
                    pltpu.make_async_remote_copy(
                        src_ref=src,
                        dst_ref=dst,
                        send_sem=fine_send.at[which, no],
                        recv_sem=fine_recv.at[which, no],
                        device_id=(c - d, a - e),
                        device_id_type=MESH,
                    ),
                )
            )
        return copies

    def coarse_copies(which):
        fields = (pl.ds(2, 1), pl.ds(0, 2), pl.ds(3, 1))[which]
        copies = []
        for no, (d, e) in enumerate(COARSE_SIDES):
            put = pl.ds({0: 0, 1: 16, -1: 32}[e], 16)
            if d == 0:
                src, dst = own_in.at[fields, :, pl.ds(0, 16), :], own_in.at[fields, :, put, :]
            elif abs(d) == 1:
                side = 0 if d > 0 else 1
                src, dst = near_out.at[side, fields], near_in.at[side, fields, :, put, :]
            else:
                side = 0 if d > 0 else 1
                src, dst = far_out.at[side, fields], far_in.at[side, {0: 0, 1: 1, -1: 2}[e], fields]
            copies.append(
                (
                    d,
                    e,
                    pltpu.make_async_remote_copy(
                        src_ref=src,
                        dst_ref=dst,
                        send_sem=coarse_send.at[which, no],
                        recv_sem=coarse_recv.at[which, no],
                        device_id=(c - d, a - e),
                        device_id_type=MESH,
                    ),
                )
            )
        return copies

    def fresh_copies():
        copies = []
        for no, (e, take) in enumerate([(1, 0), (-1, 8)]):
            copies.append(
                (
                    0,
                    e,
                    pltpu.make_async_remote_copy(
                        src_ref=grid[3].forcing.at[0, :, pl.ds(take, 8), :],
                        dst_ref=fresh.at[no],
                        send_sem=fresh_send.at[no],
                        recv_sem=fresh_recv.at[no],
                        device_id=(c, a - e),
                        device_id_type=MESH,
                    ),
                )
            )
        return copies

    def start(copies):
        for d, e, copy in copies:
            pl.when(inside(-d, -e))(copy.start)

    def arrive(copies):
        for d, e, copy in copies:
            pl.when(inside(d, e))(copy.wait_recv)

    def leave(copies):
        for d, e, copy in copies:
            pl.when(inside(-d, -e))(copy.wait_send)

    def whole_cells(which, target):
        lane = lanes_of(FINE_ROWS)
        own = lanes_of(16) < 64
        for group in range(2):
            halos = []
            for phase in range(4):
                first, last = first_in[which, phase // 2, group], last_in[which, phase // 2, group]
                if phase % 2 == 0:
                    halos.append(jnp.where(lane < 56, first, turned(last, 58)))
                else:
                    halos.append(jnp.where(lane < 56, turned(first, 64), turned(last, -6)))
            for q in range(8):
                k = 8 * group + q
                for phase in range(4):
                    edges = turned(halos[phase], 64 - 7 * q)
                    values = dense[which, phase // 2, k, 16:32]
                    values = turned(values, 64) if phase % 2 else values
                    target[phase, k, 0:16] = jnp.where(own, target[phase, k, 0:16], edges[0:16])
                    target[phase, k, 16:32] = jnp.where(own, values, edges[16:32])

    own_cells(1, cells)
    counted = (
        (jnp.minimum(c, 2) + jnp.minimum(cross_count - 1 - c, 2) + 1) * (jnp.minimum(a, 1) + jnp.minimum(along_count - 1 - a, 1) + 1) - 1
    )
    pl.semaphore_wait(barrier, counted)
    density_copies = fine_copies(1)
    start(density_copies)
    own_cells(0, grid[0].forcing)
    source_copies = fine_copies(0)
    start(source_copies)
    lane = lanes_of(FINE_ROWS)
    lane_16 = lanes_of(16)

    def pack(field, layer_of):
        near_index = 4 * (lane_16 & 15)
        far_index = 16 * ((lane_16 >> 2) & 7) + (lane_16 & 3) + 12 * (lane_16 >> 6)
        slot = lane_16 >> 4
        fars = []
        for group in range(2):
            near = jnp.zeros((16, LANES), jnp.float32)
            for q in range(8):
                near = jnp.where(slot == q, picked(layer_of(8 * group + q), near_index), near)
            own_in[field, group, 0:16] = near
            near_out[0, field, group] = turned(near, 16)
            near_out[1, field, group] = turned(near, -16)
            fars.append(picked(near, far_index))
        far = jnp.where((lane_16 & 63) < 32, fars[0], fars[1])
        low = lanes_of(8) < 64
        far_out[0, field] = jnp.where(low, far[0:8], turned(far[8:16], 64))
        far_out[1, field] = jnp.where(low, turned(far[0:8], 64), far[8:16])

    def own_upper(k):
        total = jnp.zeros((16, LANES), jnp.float32)
        for half in range(2):
            now = dense[1, half, k, 0:16]
            total += harmonic(vertical_weight, now, dense[1, half, k - 1, 0:16]) if k else 2.0 * vertical_weight * now
        return paired_lanes(paired_lanes(total + turned(total, 64), 1), 2)

    pack(2, own_upper)
    upper_copies = coarse_copies(0)
    start(upper_copies)
    for level in grid:
        level.close_upper()
    arrive(density_copies)
    whole_cells(1, cells)

    def faces(k, above):
        now = [cells[phase, k] for phase in range(4)]
        west, south, upper = [], [], []
        for phase in range(4):
            before = now[phase - 1] if phase else turned(now[3], 1)
            west.append(harmonic(along_weight, now[phase], row_turned(now[phase], 1)))
            south.append(harmonic(cross_weight, now[phase], before))
            upper.append(harmonic(vertical_weight, now[phase], above[phase]))
        upper = [jnp.where(k == 0, 2.0 * vertical_weight * now[phase], upper[phase]) for phase in range(4)]
        grid[0].set_faces(k, west, south, upper)
        west, south, upper = [west[0] + west[1], west[2] + west[3]], [0.5 * south[0], 0.5 * south[2]], [upper[0] + upper[1], upper[2] + upper[3]]
        grid[1].set_faces(k, west, south, upper)
        west, south, upper = [west[0] + west[1]], [0.5 * south[0]], [upper[0] + upper[1]]
        grid[2].set_faces(k, west, south, upper)
        west, south, upper = paired_lanes(west[0], 1), 0.5 * south[0], paired_lanes(upper[0], 1)
        grid[3].set_faces(k, [west], [south], [upper])
        return tuple(now)

    layers(faces, (jnp.ones((FINE_ROWS, LANES), jnp.float32),) * 4)

    pack(0, lambda k: paired_lanes(grid[3].west[0, k, 0:16], 2))
    pack(1, lambda k: 0.5 * grid[3].south[0, k, 0:16])
    face_copies = coarse_copies(1)
    start(face_copies)

    factor(grid[:4], centre)

    arrive(source_copies)
    whole_cells(0, grid[0].forcing)

    def restrict(no):
        level, below = grid[no], grid[no + 1]

        def after(k, values):
            rest = level.remain(k, values)
            if level.phases > 1:
                for phase in range(below.phases):
                    below.forcing[phase, k] = rest[2 * phase] + rest[2 * phase + 1]
            else:
                below.forcing[0, k] = paired_lanes(rest[0], level.spread)

        return after

    for no in (0, 1, 2):
        grid[no].start(held, restrict(no))
    third_copies = fresh_copies()
    start(third_copies)

    def keep_rest(k, values):
        cells[0, k] = grid[3].remain(k, values)[0]

    grid[3].start(held, keep_rest)
    pack(3, lambda k: paired_lanes(cells[0, k, 0:16], 2))
    forcing_copies = coarse_copies(2)
    start(forcing_copies)

    arrive(third_copies)

    def renew(k, _):
        grid[3].forcing[0, k, 16:24] = fresh[0, k]
        grid[3].forcing[0, k, 24:32] = fresh[1, k]
        return 0

    layers(renew, 0)
    grid[3].start(held, low=16)

    lane_8, lane_24 = lanes_of(8), lanes_of(COARSE_ROWS)

    def unpacked(field):
        slot_8, part_8, inner = lane_8 >> 4, lane_8 & 3, (lane_8 & 15) < 8

        def far(side, no, half, group, shift):
            return picked(far_in[side, no, field], 64 * half + 4 * (8 * group + ((slot_8 - shift) & 7)) + part_8)

        tiles = [((2, 0), (0, 1)), ((2, 1), (1, 0)), ((0, 0), (1, 1))]
        sources = []
        for group in range(2):
            places = {}
            for place, ref in ((0, own_in.at[field, group]), (1, near_in.at[0, field, group]), (7, near_in.at[1, field, group])):
                places[place] = jnp.concatenate([ref[32:48], ref[0:8]], 0)
                places[(place + 4) % 8] = turned(ref[8:32], 64)
            places[2] = jnp.concatenate([jnp.where(inner, far(0, *lower, group, 2), far(1, *higher, group, 2)) for lower, higher in tiles], 0)
            places[6] = jnp.concatenate([jnp.where(inner, far(0, *higher, group, 6), far(1, *lower, group, 6)) for lower, higher in tiles], 0)
            sources.append(places)
        slot = lane_24 >> 4

        def layer_of(k):
            places, q = sources[k // 8], k % 8
            at = (slot - q) & 7
            mixed = places[0]
            for place in range(1, 8):
                mixed = jnp.where(at == place, places[place], mixed)
            return turned(mixed, 24 - 16 * q)

        return layer_of

    arrive(upper_copies)
    arrive(face_copies)
    west_of, south_of, upper_of = unpacked(0), unpacked(1), unpacked(2)
    for k in range(NZ):
        west, south, upper = west_of(k), south_of(k), upper_of(k)
        grid[4].set_faces(k, [west], [south], [upper])
        for no in (5, 6):
            spread = grid[no].spread // 2
            west, south, upper = paired_lanes(west, spread), 0.5 * south, paired_lanes(upper, spread)
            grid[no].set_faces(k, [west], [south], [upper])
    factor(grid[4:])
    for level in grid[:3]:
        level.near()

    arrive(forcing_copies)
    forcing_of = unpacked(3)
    for k in range(NZ):
        grid[4].forcing[0, k] = forcing_of(k)

    grid[4].start(coarse_held, restrict(4))
    grid[5].start(coarse_held, restrict(5))
    grid[6].start(coarse_held)
    for _ in range(SWEEPS - 1):
        grid[6].sweep(coarse_held)
    grid[5].sweep(coarse_held, lambda k: [both_children(grid[6].value[0, k], 2, lane_24)])
    grid[4].sweep(coarse_held, lambda k: [both_children(grid[5].value[0, k], 1, lane_24)])

    row = lax.broadcasted_iota(jnp.int32, (FINE_ROWS, LANES), 0)
    third_index = jnp.where(lane < 96, (lane >> 2) + 24, (lane >> 2) - 8) + jnp.where((row >= 8) & (row < 24), 64, 0)

    def to_third(k):
        values = grid[4].value[0, k]
        return [picked(jnp.concatenate([values[16:24], values[0:16], values[8:16]], 0), third_index)]

    grid[3].sweep(held, to_third)
    first = lax.broadcasted_iota(jnp.int32, (8, LANES), 0) < 4

    def to_second(k):
        values = grid[3].value[0, k]
        values = jnp.concatenate([values[0:16], jnp.where(first, values[16:24], values[24:32])], 0)
        return [both_children(values, 1, lane_24)]

    grid[2].sweep(held, to_second)
    grid[1].sweep(held, lambda k: [grid[2].value[0, k, 0:24]] * 2)
    def laid_out(ref, k, phases):
        halves = [jnp.where(lane_16 < 64, phases[2 * half], turned(phases[2 * half + 1], 64)) for half in range(2)]
        index = (lane_16 & 1) * 64 + (lane_16 >> 2)
        for tile in range(2):
            at = index + 32 * tile
            ref[k, :, tile * LANES : (tile + 1) * LANES] = jnp.where((lane_16 & 3) < 2, picked(halves[0], at), picked(halves[1], at))

    fine = grid[0]
    grid[0].sweep(held, lambda k: [grid[1].value[phase // 2, k, 0:24] for phase in range(4)], lambda k, values: laid_out(pressure_ref, k, [value[0:16] for value in values]))

    def finish(k, above):
        values = [fine.value[phase, k, 0:24] for phase in range(4)]
        next_k = jnp.minimum(k + 1, NZ - 1)
        rest = []
        for phase, part in enumerate(fine.horizontal(k, values)):
            own = pl.ds(0, 16)
            below = fine.value[phase, next_k, own]
            rest.append(
                fine.forcing[phase, k, own]
                - (
                    centre[phase, k, own] * values[phase][0:16]
                    - part[0:16]
                    - fine.upper[phase, k, own] * above[phase]
                    - fine.upper[phase, k + 1, own] * below
                )
            )
        values = [value[0:16] for value in values]
        laid_out(residual_ref, k, rest)
        return tuple(values)

    layers(finish, (jnp.zeros((16, LANES), jnp.float32),) * 4)

    for copies in (density_copies, source_copies, upper_copies, face_copies, third_copies, forcing_copies):
        leave(copies)


def solution(mesh):
    cross_count, along_count = mesh.shape["cross"], mesh.shape["along"]

    def per_device(source, density):
        shape = jax.ShapeDtypeStruct(source.shape, jnp.float32)
        vmem = lambda *dims: pltpu.VMEM(dims, jnp.float32)
        scratch = [
            vmem(2, *source.shape),
            vmem(2, 2, NZ, FINE_ROWS, LANES),
            vmem(2, 2, 2, 16, LANES),
            vmem(2, 2, 2, 16, LANES),
            vmem(2, 2, 2, FINE_ROWS, LANES),
            vmem(2, 2, 2, FINE_ROWS, LANES),
            vmem(2, 4, 2, 16, LANES),
            vmem(2, 4, 8, LANES),
            vmem(4, 2, HELD_ROWS, LANES),
            vmem(2, 4, 2, HELD_ROWS, LANES),
            vmem(2, 3, 4, 8, LANES),
            vmem(2, NZ, 8, LANES),
            vmem(4, NZ, FINE_ROWS, LANES),
            vmem(4, NZ, FINE_ROWS, LANES),
            vmem(4, NZ, FINE_ROWS, LANES),
            vmem(1, NZ, COARSE_ROWS, LANES),
        ]
        for phases, rows in [(4, FINE_ROWS), (2, FINE_ROWS), (1, FINE_ROWS), (1, FINE_ROWS)] + [(1, COARSE_ROWS)] * 3:
            scratch += Level.scratch(phases, rows)
        scratch += [
            pltpu.SemaphoreType.DMA((2,)),
            pltpu.SemaphoreType.DMA((2, len(FINE_SIDES))),
            pltpu.SemaphoreType.DMA((2, len(FINE_SIDES))),
            pltpu.SemaphoreType.DMA((3, len(COARSE_SIDES))),
            pltpu.SemaphoreType.DMA((3, len(COARSE_SIDES))),
            pltpu.SemaphoreType.DMA((2,)),
            pltpu.SemaphoreType.DMA((2,)),
        ]
        pressure, residual = pl.pallas_call(
            functools.partial(kernel, cross_count, along_count),
            out_shape=(pltpu.VMEM(shape.shape, shape.dtype),) * 2,
            in_specs=[pl.BlockSpec(memory_space=pl.ANY)] * 2,
            out_specs=(pl.BlockSpec(memory_space=pltpu.VMEM),) * 2,
            scratch_shapes=scratch,
            compiler_params=pltpu.CompilerParams(collective_id=0, has_side_effects=True, vmem_limit_bytes=56 * 2**20),
        )(source, density)
        return pressure, residual

    return jax.shard_map(
        per_device,
        mesh=mesh,
        in_specs=(P(None, "along", "cross"), P(None, "along", "cross")),
        out_specs=(P(None, "along", "cross"), P(None, "along", "cross")),
        check_vma=False,
    )
```

```python
import functools

import jax
import jax.numpy as jnp
from jax import lax
from jax.experimental import pallas as pl
from jax.experimental.pallas import tpu as pltpu
from jax.sharding import PartitionSpec as P

MESH = pl.DeviceIdType.MESH
SWEEPS = 4
NZ = 16
LANES = 128
FINE_ROWS = 32
COARSE_ROWS = 24
HELD_ROWS = 48
TINY = 1e-20

along_weight = 0.25
cross_weight = 1.0
vertical_weight = 0.5
relaxation = 0.8

COARSE_SIDES = [(d, e) for d in (2, -2, 1, -1, 0) for e in (0, 1, -1) if (d, e) != (0, 0)]
FINE_SIDES = [(d, e) for d in (1, -1, 0) for e in (0, 1, -1) if (d, e) != (0, 0)]


def layers(body, init, reverse=False):
    def step(i, carry):
        return body(NZ - 1 - i if reverse else i, carry)

    return lax.fori_loop(0, NZ, step, init, unroll=True)


def picked(values, lane_index):
    return jnp.take_along_axis(values, lane_index, axis=1, mode="promise_in_bounds")


def turned(values, by):
    return pltpu.roll(values, by % LANES, axis=1)


def row_turned(values, by):
    return pltpu.roll(values, by % values.shape[0], axis=0)


def harmonic(weight, first, second):
    product = first * second if weight == 0.5 else (2.0 * weight) * first * second
    return product * (1.0 / (first + second))


def lanes_of(rows):
    return lax.broadcasted_iota(jnp.int32, (rows, LANES), 1)


def row_before(values, folded):
    moved = row_turned(values, 1)
    if not folded:
        return moved
    head = moved[0:8]
    first = lax.broadcasted_iota(jnp.int32, head.shape, 0) == 0
    return jnp.concatenate([jnp.where(first, turned(head, 64), head), moved[8:]], 0)


def row_after(values, folded):
    moved = row_turned(values, -1)
    if not folded:
        return moved
    tail = moved[-8:]
    last = lax.broadcasted_iota(jnp.int32, tail.shape, 0) == 7
    return jnp.concatenate([moved[:-8], jnp.where(last, turned(tail, 64), tail)], 0)


class Level:
    def __init__(self, phases, spread, rows, refs):
        self.phases, self.spread, self.rows, self.folded = phases, spread, rows, rows == COARSE_ROWS
        self.west, self.south, self.upper, self.gain, self.pull, self.link, self.value, self.forcing = refs

    @staticmethod
    def scratch(phases, rows):
        full = pltpu.VMEM((phases, NZ, rows, LANES), jnp.float32)
        column = pltpu.VMEM((phases, NZ + 1, rows, LANES), jnp.float32)
        return [full, full, column, full, full, full, full, full]

    def horizontal(self, k, values):
        rows = pl.ds(0, values[0].shape[0])
        west = [self.west[phase, k, rows] for phase in range(self.phases)]
        south = [self.south[phase, k, rows] for phase in range(self.phases)]
        onward = [face * value for face, value in zip(south, values)]
        out = []
        for phase, value in enumerate(values):
            before = values[phase - 1] if phase else turned(values[-1], self.spread)
            north = onward[phase + 1] if phase + 1 < self.phases else turned(onward[0], -self.spread)
            along = west[phase] * row_before(value, self.folded) + row_after(west[phase] * value, self.folded)
            out.append(along + south[phase] * before + north)
        return out

    def set_faces(self, k, west, south, upper):
        for phase in range(self.phases):
            self.west[phase, k] = west[phase]
            self.south[phase, k] = south[phase]
            self.upper[phase, k] = upper[phase]

    def close_upper(self):
        for phase in range(self.phases):
            self.upper[phase, NZ] = jnp.zeros((self.rows, LANES), jnp.float32)

    def start(self, held, after=None, low=0):
        rows = pl.ds(low, self.rows - low)
        zero = jnp.zeros((self.rows - low, LANES), jnp.float32)

        def down(k, before):
            now = []
            for phase in range(self.phases):
                now.append(self.gain[phase, k, rows] * self.forcing[phase, k, rows] + self.pull[phase, k, rows] * before[phase])
                held[phase, k, rows] = now[-1]
            return tuple(now)

        layers(down, (zero,) * self.phases)

        def up(k, below):
            values = []
            for phase in range(self.phases):
                values.append(held[phase, k, rows] + self.link[phase, k, rows] * below[phase])
                self.value[phase, k, rows] = values[-1]
            if after is not None:
                after(k, values)
            return tuple(values)

        layers(up, (zero,) * self.phases, reverse=True)

    def remain(self, k, values):
        return [(1.0 - relaxation) * self.forcing[phase, k] + part for phase, part in enumerate(self.horizontal(k, values))]

    def near(self):
        first = lax.broadcasted_iota(jnp.int32, (8, LANES), 0) < 4

        def body(k, _):
            for ref in (self.west, self.south, self.gain, self.pull, self.link, self.value, self.forcing):
                for phase in range(self.phases):
                    ref[phase, k, 16:24] = jnp.where(first, ref[phase, k, 16:24], ref[phase, k, 24:32])
            return 0

        layers(body, 0)
        self.rows = 24

    def sweep(self, held, coarse=None, after=None):
        zero = jnp.zeros((self.rows, LANES), jnp.float32)
        rows = pl.ds(0, self.rows)

        def down(k, before):
            values = [self.value[phase, k, rows] for phase in range(self.phases)]
            if coarse is not None:
                values = [value + extra for value, extra in zip(values, coarse(k))]
                for phase in range(self.phases):
                    self.value[phase, k, rows] = values[phase]
            now = []
            for phase, part in enumerate(self.horizontal(k, values)):
                now.append(self.gain[phase, k, rows] * (self.forcing[phase, k, rows] + part) + self.pull[phase, k, rows] * before[phase])
                held[phase, k, rows] = now[-1]
            return tuple(now)

        layers(down, (zero,) * self.phases)

        def up(k, below):
            now, values = [], []
            for phase in range(self.phases):
                now.append(held[phase, k, rows] + self.link[phase, k, rows] * below[phase])
                values.append((1.0 - relaxation) * self.value[phase, k, rows] + now[-1])
                self.value[phase, k, rows] = values[-1]
            if after is not None:
                after(k, values)
            return tuple(now)

        layers(up, (zero,) * self.phases, reverse=True)


def factor(levels, centre_ref=None):
    def body(k, before):
        now = []
        for no, level in enumerate(levels):
            links = []
            for phase in range(level.phases):
                upper, lower = level.upper[phase, k], level.upper[phase, k + 1]
                west, south = level.west[phase, k], level.south[phase, k]
                north = level.south[phase + 1, k] if phase + 1 < level.phases else turned(level.south[0, k], -level.spread)
                centre = west + row_after(west, level.folded) + south + north + upper + lower
                if no == 0 and centre_ref is not None:
                    centre_ref[phase, k] = centre
                inverse = 1.0 / jnp.maximum(centre - upper * before[no][phase], TINY)
                level.gain[phase, k] = relaxation * inverse
                level.pull[phase, k] = upper * inverse
                links.append(lower * inverse)
                level.link[phase, k] = links[-1]
            now.append(tuple(links))
        return tuple(now)

    layers(body, tuple((jnp.zeros((level.rows, LANES), jnp.float32),) * level.phases for level in levels))


def paired_lanes(values, spread):
    return values + turned(values, -spread)


def both_children(values, spread, lane):
    return jnp.where((lane & spread) == 0, values, turned(values, spread))


def kernel(
    cross_count,
    along_count,
    source_hbm,
    density_hbm,
    pressure_ref,
    residual_ref,
    raw,
    dense,
    first_out,
    last_out,
    first_in,
    last_in,
    near_out,
    far_out,
    own_in,
    near_in,
    far_in,
    fresh,
    cells,
    centre,
    held,
    coarse_held,
    *rest,
):
    level_refs, (own_sem, fine_send, fine_recv, coarse_send, coarse_recv, fresh_send, fresh_recv) = rest[:-7], rest[-7:]
    shapes = [(4, 1, FINE_ROWS), (2, 1, FINE_ROWS), (1, 1, FINE_ROWS), (1, 2, FINE_ROWS), (1, 1, COARSE_ROWS), (1, 2, COARSE_ROWS), (1, 4, COARSE_ROWS)]
    grid = [Level(*shape, level_refs[8 * no : 8 * no + 8]) for no, shape in enumerate(shapes)]
    c, a = lax.axis_index("cross"), lax.axis_index("along")

    def inside(d, e):
        return (c + d >= 0) & (c + d < cross_count) & (a + e >= 0) & (a + e < along_count)

    own_copies = [pltpu.make_async_copy(hbm, raw.at[which], own_sem.at[which]) for which, hbm in ((0, source_hbm), (1, density_hbm))]
    for copy in own_copies[::-1]:
        copy.start()

    @pl.when((c < 2) | (c > cross_count - 3) | (a < 1) | (a > along_count - 2))
    def _():
        for ref in (own_in, near_in, far_in, fresh):
            ref[...] = jnp.zeros(ref.shape, ref.dtype)
        dense[0, :, :, 16:32, :] = jnp.zeros((2, NZ, 16, LANES), jnp.float32)
        dense[1, :, :, 16:32, :] = jnp.full((2, NZ, 16, LANES), TINY, jnp.float32)
        for ref in (first_in, last_in):
            ref[0] = jnp.zeros(ref.shape[1:], ref.dtype)
            ref[1] = jnp.full(ref.shape[1:], TINY, ref.dtype)

    barrier = pltpu.get_barrier_semaphore()
    for d, e in COARSE_SIDES:

        @pl.when(inside(d, e))
        def _(d=d, e=e):
            pl.semaphore_signal(barrier, inc=1, device_id=(c + d, a + e), device_id_type=MESH)

    def own_cells(which, target):
        own_copies[which].wait()
        ref = raw.at[which]
        lane = lanes_of(16)
        index = (4 * (lane & 63) + (lane >> 6)) & 127
        lower = (lane & 63) < 32

        def body(k, _):
            left, right = ref[k, :, 0:LANES], ref[k, :, LANES : 2 * LANES]
            for half in range(2):
                at = index + 2 * half
                values = jnp.where(lower, picked(left, at), picked(right, at))
                dense[which, half, k, 0:16] = values
                target[2 * half, k, 0:16] = values
                target[2 * half + 1, k, 0:16] = turned(values, 64)
            return 0

        layers(body, 0)
        part = lane & 63
        for half in range(2):
            for group in range(2):
                first = last = jnp.zeros((16, LANES), jnp.float32)
                for q in range(8):
                    values = dense[which, half, 8 * group + q, 0:16]
                    here = (part >= 7 * q) & (part < 7 * q + 7)
                    first = jnp.where(here, turned(values, 7 * q), first)
                    last = jnp.where(here, turned(values, 7 * q - 58), last)
                first_out[which, half, group] = first
                last_out[which, half, group] = last

    def fine_copies(which):
        copies = []
        for no, (d, e) in enumerate(FINE_SIDES):
            rows_from = {0: (0, 16), 1: (0, 8), -1: (8, 16)}[e]
            rows_to = {0: (0, 16), 1: (16, 24), -1: (24, 32)}[e]
            take, put = pl.ds(rows_from[0], rows_from[1] - rows_from[0]), pl.ds(rows_to[0], rows_to[1] - rows_to[0])
            if d == 0:
                src, dst = dense.at[which, :, :, take, :], dense.at[which, :, :, put, :]
            elif d == 1:
                src, dst = first_out.at[which, :, :, take, :], first_in.at[which, :, :, put, :]
            else:
                src, dst = last_out.at[which, :, :, take, :], last_in.at[which, :, :, put, :]
            copies.append(
                (
                    d,
                    e,
                    pltpu.make_async_remote_copy(
                        src_ref=src,
                        dst_ref=dst,
                        send_sem=fine_send.at[which, no],
                        recv_sem=fine_recv.at[which, no],
                        device_id=(c - d, a - e),
                        device_id_type=MESH,
                    ),
                )
            )
        return copies

    def coarse_copies(which):
        fields = (pl.ds(2, 1), pl.ds(0, 2), pl.ds(3, 1))[which]
        copies = []
        for no, (d, e) in enumerate(COARSE_SIDES):
            put = pl.ds({0: 0, 1: 16, -1: 32}[e], 16)
            if d == 0:
                src, dst = own_in.at[fields, :, pl.ds(0, 16), :], own_in.at[fields, :, put, :]
            elif abs(d) == 1:
                side = 0 if d > 0 else 1
                src, dst = near_out.at[side, fields], near_in.at[side, fields, :, put, :]
            else:
                side = 0 if d > 0 else 1
                src, dst = far_out.at[side, fields], far_in.at[side, {0: 0, 1: 1, -1: 2}[e], fields]
            copies.append(
                (
                    d,
                    e,
                    pltpu.make_async_remote_copy(
                        src_ref=src,
                        dst_ref=dst,
                        send_sem=coarse_send.at[which, no],
                        recv_sem=coarse_recv.at[which, no],
                        device_id=(c - d, a - e),
                        device_id_type=MESH,
                    ),
                )
            )
        return copies

    def fresh_copies():
        copies = []
        for no, (e, take) in enumerate([(1, 0), (-1, 8)]):
            copies.append(
                (
                    0,
                    e,
                    pltpu.make_async_remote_copy(
                        src_ref=grid[3].forcing.at[0, :, pl.ds(take, 8), :],
                        dst_ref=fresh.at[no],
                        send_sem=fresh_send.at[no],
                        recv_sem=fresh_recv.at[no],
                        device_id=(c, a - e),
                        device_id_type=MESH,
                    ),
                )
            )
        return copies

    def start(copies):
        for d, e, copy in copies:
            pl.when(inside(-d, -e))(copy.start)

    def arrive(copies):
        for d, e, copy in copies:
            pl.when(inside(d, e))(copy.wait_recv)

    def leave(copies):
        for d, e, copy in copies:
            pl.when(inside(-d, -e))(copy.wait_send)

    def whole_cells(which, target):
        lane = lanes_of(FINE_ROWS)
        own = lanes_of(16) < 64
        for group in range(2):
            halos = []
            for phase in range(4):
                first, last = first_in[which, phase // 2, group], last_in[which, phase // 2, group]
                if phase % 2 == 0:
                    halos.append(jnp.where(lane < 56, first, turned(last, 58)))
                else:
                    halos.append(jnp.where(lane < 56, turned(first, 64), turned(last, -6)))
            for q in range(8):
                k = 8 * group + q
                for phase in range(4):
                    edges = turned(halos[phase], 64 - 7 * q)
                    values = dense[which, phase // 2, k, 16:32]
                    values = turned(values, 64) if phase % 2 else values
                    target[phase, k, 0:16] = jnp.where(own, target[phase, k, 0:16], edges[0:16])
                    target[phase, k, 16:32] = jnp.where(own, values, edges[16:32])

    own_cells(1, cells)
    counted = (
        (jnp.minimum(c, 2) + jnp.minimum(cross_count - 1 - c, 2) + 1) * (jnp.minimum(a, 1) + jnp.minimum(along_count - 1 - a, 1) + 1) - 1
    )
    pl.semaphore_wait(barrier, counted)
    density_copies = fine_copies(1)
    start(density_copies)
    own_cells(0, grid[0].forcing)
    source_copies = fine_copies(0)
    start(source_copies)
    lane = lanes_of(FINE_ROWS)
    lane_16 = lanes_of(16)

    def pack(field, layer_of):
        near_index = 4 * (lane_16 & 15)
        far_index = 16 * ((lane_16 >> 2) & 7) + (lane_16 & 3) + 12 * (lane_16 >> 6)
        slot = lane_16 >> 4
        fars = []
        for group in range(2):
            near = jnp.zeros((16, LANES), jnp.float32)
            for q in range(8):
                near = jnp.where(slot == q, picked(layer_of(8 * group + q), near_index), near)
            own_in[field, group, 0:16] = near
            near_out[0, field, group] = turned(near, 16)
            near_out[1, field, group] = turned(near, -16)
            fars.append(picked(near, far_index))
        far = jnp.where((lane_16 & 63) < 32, fars[0], fars[1])
        low = lanes_of(8) < 64
        far_out[0, field] = jnp.where(low, far[0:8], turned(far[8:16], 64))
        far_out[1, field] = jnp.where(low, turned(far[0:8], 64), far[8:16])

    def own_upper(k):
        total = jnp.zeros((16, LANES), jnp.float32)
        for half in range(2):
            now = dense[1, half, k, 0:16]
            total += harmonic(vertical_weight, now, dense[1, half, k - 1, 0:16]) if k else 2.0 * vertical_weight * now
        return paired_lanes(paired_lanes(total + turned(total, 64), 1), 2)

    pack(2, own_upper)
    upper_copies = coarse_copies(0)
    start(upper_copies)
    for level in grid:
        level.close_upper()
    arrive(density_copies)
    whole_cells(1, cells)

    def faces(k, above):
        now = [cells[phase, k] for phase in range(4)]
        west, south, upper = [], [], []
        for phase in range(4):
            before = now[phase - 1] if phase else turned(now[3], 1)
            west.append(harmonic(along_weight, now[phase], row_turned(now[phase], 1)))
            south.append(harmonic(cross_weight, now[phase], before))
            upper.append(harmonic(vertical_weight, now[phase], above[phase]))
        upper = [jnp.where(k == 0, 2.0 * vertical_weight * now[phase], upper[phase]) for phase in range(4)]
        grid[0].set_faces(k, west, south, upper)
        west, south, upper = [west[0] + west[1], west[2] + west[3]], [0.5 * south[0], 0.5 * south[2]], [upper[0] + upper[1], upper[2] + upper[3]]
        grid[1].set_faces(k, west, south, upper)
        west, south, upper = [west[0] + west[1]], [0.5 * south[0]], [upper[0] + upper[1]]
        grid[2].set_faces(k, west, south, upper)
        west, south, upper = paired_lanes(west[0], 1), 0.5 * south[0], paired_lanes(upper[0], 1)
        grid[3].set_faces(k, [west], [south], [upper])
        return tuple(now)

    layers(faces, (jnp.ones((FINE_ROWS, LANES), jnp.float32),) * 4)

    pack(0, lambda k: paired_lanes(grid[3].west[0, k, 0:16], 2))
    pack(1, lambda k: 0.5 * grid[3].south[0, k, 0:16])
    face_copies = coarse_copies(1)
    start(face_copies)

    factor(grid[:4], centre)

    arrive(source_copies)
    whole_cells(0, grid[0].forcing)

    def restrict(no):
        level, below = grid[no], grid[no + 1]

        def after(k, values):
            rest = level.remain(k, values)
            if level.phases > 1:
                for phase in range(below.phases):
                    below.forcing[phase, k] = rest[2 * phase] + rest[2 * phase + 1]
            else:
                below.forcing[0, k] = paired_lanes(rest[0], level.spread)

        return after

    for no in (0, 1, 2):
        grid[no].start(held, restrict(no))
    third_copies = fresh_copies()
    start(third_copies)

    def keep_rest(k, values):
        cells[0, k] = grid[3].remain(k, values)[0]

    grid[3].start(held, keep_rest)
    pack(3, lambda k: paired_lanes(cells[0, k, 0:16], 2))
    forcing_copies = coarse_copies(2)
    start(forcing_copies)

    arrive(third_copies)

    def renew(k, _):
        grid[3].forcing[0, k, 16:24] = fresh[0, k]
        grid[3].forcing[0, k, 24:32] = fresh[1, k]
        return 0

    layers(renew, 0)
    grid[3].start(held, low=16)

    lane_8, lane_24 = lanes_of(8), lanes_of(COARSE_ROWS)

    def unpacked(field):
        slot_8, part_8, inner = lane_8 >> 4, lane_8 & 3, (lane_8 & 15) < 8

        def far(side, no, half, group, shift):
            return picked(far_in[side, no, field], 64 * half + 4 * (8 * group + ((slot_8 - shift) & 7)) + part_8)

        tiles = [((2, 0), (0, 1)), ((2, 1), (1, 0)), ((0, 0), (1, 1))]
        sources = []
        for group in range(2):
            places = {}
            for place, ref in ((0, own_in.at[field, group]), (1, near_in.at[0, field, group]), (7, near_in.at[1, field, group])):
                places[place] = jnp.concatenate([ref[32:48], ref[0:8]], 0)
                places[(place + 4) % 8] = turned(ref[8:32], 64)
            places[2] = jnp.concatenate([jnp.where(inner, far(0, *lower, group, 2), far(1, *higher, group, 2)) for lower, higher in tiles], 0)
            places[6] = jnp.concatenate([jnp.where(inner, far(0, *higher, group, 6), far(1, *lower, group, 6)) for lower, higher in tiles], 0)
            sources.append(places)
        slot = lane_24 >> 4

        def layer_of(k):
            places, q = sources[k // 8], k % 8
            at = (slot - q) & 7
            mixed = places[0]
            for place in range(1, 8):
                mixed = jnp.where(at == place, places[place], mixed)
            return turned(mixed, 24 - 16 * q)

        return layer_of

    arrive(upper_copies)
    arrive(face_copies)
    west_of, south_of, upper_of = unpacked(0), unpacked(1), unpacked(2)
    for k in range(NZ):
        west, south, upper = west_of(k), south_of(k), upper_of(k)
        grid[4].set_faces(k, [west], [south], [upper])
        for no in (5, 6):
            spread = grid[no].spread // 2
            west, south, upper = paired_lanes(west, spread), 0.5 * south, paired_lanes(upper, spread)
            grid[no].set_faces(k, [west], [south], [upper])
    factor(grid[4:])
    for level in grid[:3]:
        level.near()

    for copies in (density_copies, source_copies, upper_copies, face_copies, third_copies):
        leave(copies)
    arrive(forcing_copies)
    forcing_of = unpacked(3)
    for k in range(NZ):
        grid[4].forcing[0, k] = forcing_of(k)

    grid[4].start(coarse_held, restrict(4))
    grid[5].start(coarse_held, restrict(5))
    grid[6].start(coarse_held)
    for _ in range(SWEEPS - 1):
        grid[6].sweep(coarse_held)
    grid[5].sweep(coarse_held, lambda k: [both_children(grid[6].value[0, k], 2, lane_24)])
    grid[4].sweep(coarse_held, lambda k: [both_children(grid[5].value[0, k], 1, lane_24)])

    row = lax.broadcasted_iota(jnp.int32, (FINE_ROWS, LANES), 0)
    third_index = jnp.where(lane < 96, (lane >> 2) + 24, (lane >> 2) - 8) + jnp.where((row >= 8) & (row < 24), 64, 0)

    def to_third(k):
        values = grid[4].value[0, k]
        return [picked(jnp.concatenate([values[16:24], values[0:16], values[8:16]], 0), third_index)]

    grid[3].sweep(held, to_third)
    first = lax.broadcasted_iota(jnp.int32, (8, LANES), 0) < 4

    def to_second(k):
        values = grid[3].value[0, k]
        values = jnp.concatenate([values[0:16], jnp.where(first, values[16:24], values[24:32])], 0)
        return [both_children(values, 1, lane_24)]

    grid[2].sweep(held, to_second)
    grid[1].sweep(held, lambda k: [grid[2].value[0, k, 0:24]] * 2)
    def laid_out(ref, k, phases):
        halves = [jnp.where(lane_16 < 64, phases[2 * half], turned(phases[2 * half + 1], 64)) for half in range(2)]
        index = (lane_16 & 1) * 64 + (lane_16 >> 2)
        for tile in range(2):
            at = index + 32 * tile
            ref[k, :, tile * LANES : (tile + 1) * LANES] = jnp.where((lane_16 & 3) < 2, picked(halves[0], at), picked(halves[1], at))

    fine = grid[0]
    grid[0].sweep(held, lambda k: [grid[1].value[phase // 2, k, 0:24] for phase in range(4)], lambda k, values: laid_out(pressure_ref, k, [value[0:16] for value in values]))

    def finish(k, above):
        values = [fine.value[phase, k, 0:24] for phase in range(4)]
        next_k = jnp.minimum(k + 1, NZ - 1)
        rest = []
        for phase, part in enumerate(fine.horizontal(k, values)):
            own = pl.ds(0, 16)
            below = fine.value[phase, next_k, own]
            rest.append(
                fine.forcing[phase, k, own]
                - (
                    centre[phase, k, own] * values[phase][0:16]
                    - part[0:16]
                    - fine.upper[phase, k, own] * above[phase]
                    - fine.upper[phase, k + 1, own] * below
                )
            )
        values = [value[0:16] for value in values]
        laid_out(residual_ref, k, rest)
        return tuple(values)

    layers(finish, (jnp.zeros((16, LANES), jnp.float32),) * 4)

    leave(forcing_copies)


def solution(mesh):
    cross_count, along_count = mesh.shape["cross"], mesh.shape["along"]

    def per_device(source, density):
        shape = jax.ShapeDtypeStruct(source.shape, jnp.float32)
        vmem = lambda *dims: pltpu.VMEM(dims, jnp.float32)
        scratch = [
            vmem(2, *source.shape),
            vmem(2, 2, NZ, FINE_ROWS, LANES),
            vmem(2, 2, 2, 16, LANES),
            vmem(2, 2, 2, 16, LANES),
            vmem(2, 2, 2, FINE_ROWS, LANES),
            vmem(2, 2, 2, FINE_ROWS, LANES),
            vmem(2, 4, 2, 16, LANES),
            vmem(2, 4, 8, LANES),
            vmem(4, 2, HELD_ROWS, LANES),
            vmem(2, 4, 2, HELD_ROWS, LANES),
            vmem(2, 3, 4, 8, LANES),
            vmem(2, NZ, 8, LANES),
            vmem(4, NZ, FINE_ROWS, LANES),
            vmem(4, NZ, FINE_ROWS, LANES),
            vmem(4, NZ, FINE_ROWS, LANES),
            vmem(1, NZ, COARSE_ROWS, LANES),
        ]
        for phases, rows in [(4, FINE_ROWS), (2, FINE_ROWS), (1, FINE_ROWS), (1, FINE_ROWS)] + [(1, COARSE_ROWS)] * 3:
            scratch += Level.scratch(phases, rows)
        scratch += [
            pltpu.SemaphoreType.DMA((2,)),
            pltpu.SemaphoreType.DMA((2, len(FINE_SIDES))),
            pltpu.SemaphoreType.DMA((2, len(FINE_SIDES))),
            pltpu.SemaphoreType.DMA((3, len(COARSE_SIDES))),
            pltpu.SemaphoreType.DMA((3, len(COARSE_SIDES))),
            pltpu.SemaphoreType.DMA((2,)),
            pltpu.SemaphoreType.DMA((2,)),
        ]
        pressure, residual = pl.pallas_call(
            functools.partial(kernel, cross_count, along_count),
            out_shape=(pltpu.VMEM(shape.shape, shape.dtype),) * 2,
            in_specs=[pl.BlockSpec(memory_space=pl.ANY)] * 2,
            out_specs=(pl.BlockSpec(memory_space=pltpu.VMEM),) * 2,
            scratch_shapes=scratch,
            compiler_params=pltpu.CompilerParams(collective_id=0, has_side_effects=True, vmem_limit_bytes=56 * 2**20),
        )(source, density)
        return pressure, residual

    return jax.shard_map(
        per_device,
        mesh=mesh,
        in_specs=(P(None, "along", "cross"), P(None, "along", "cross")),
        out_specs=(P(None, "along", "cross"), P(None, "along", "cross")),
        check_vma=False,
    )
```
